32 devices in a mesh: groups: 2 (over x), tok: 8 (over z, y), dom: 2 (over core).
Axes of the slice: x: 2, y: 2, z: 4, core: 2. Of those that a mesh axis runs over, the one named last changes fastest.
Arguments:
- states: bfloat16 [32, 128, 768], P(('groups', 'dom'), 'tok'), parts along dimension 0, may hold values from -12 to 12
- ancestors: int32 [32], P(('groups', 'dom')), parts along dimension 0, may hold values from 0 to 15, as said below
- noise: bfloat16 [32, 128, 768], P(('groups', 'dom'), 'tok'), parts along dimension 0, may hold values from -6 to 6
- pair: bfloat16 [256, 128, 128], P(('groups', 'tok')), parts along dimension 0, may hold values from -200 to 200
- token_mask: int32 [256], P('groups'), parts along dimension 0, may hold values 0 or 1
- w_qkv: bfloat16 [2, 768, 2304], replicated, may hold values from -0.21875 to 0.21875
- w_out: bfloat16 [2, 768, 768], replicated, may hold values from -0.21875 to 0.21875
- w_pair: bfloat16 [2, 128, 16], replicated, may hold values from -1.5 to 1.5
Outputs:
- new_states: bfloat16 [32, 128, 768], P(('groups', 'dom'), 'tok'), parts along dimension 0
The draws below stay inside these ranges and needn't reach their ends.
There are 2 independent parts, one for each index of `groups`. The reference program is written for one: setup_inputs(seed, part) draws one part's arguments, and reference() takes and returns one part's arrays. A program takes and returns all parts, laid end to end along the dimension named above; an argument that names none is the same for every part. Nothing has to cross between parts.
Inputs may be any that keep to these rules, and one draw needn't show every extreme that they name: `ancestors`: nondecreasing over particles; the first entry is 0 and the last is 15.
All inputs are finite; a program needn't handle non-finite values.
Results may differ from the reference program's by a relative error of at most 0.015.
Values may be sent and summed in bfloat16 or wider, within the bound.
A program may use at most 128 MiB of HBM per device.

```python
import jax
import jax.numpy as jnp
from jax import lax

D = 768
HEADS = 16
C_PAIR = 128
LAYERS = 2
HEAD_DIM = 48
TOKENS = 128
PARTICLES = 16


def draw_states(key, part):
    key_base = jax.random.fold_in(key, 0)
    shape = (PARTICLES, TOKENS, D)
    result = jnp.clip(jax.random.normal(key_base, shape, jnp.float32), -6.0, 6.0)
    return result.astype(jnp.bfloat16)


def draw_pair(key, part):
    key_base = jax.random.fold_in(key, 0)
    shape = (TOKENS, TOKENS, C_PAIR)
    result = jnp.clip(jax.random.normal(key_base, shape, jnp.float32), -6.0, 6.0)
    return result.astype(jnp.bfloat16)


def draw_ancestors(key, part):
    picked = jnp.sort(jax.random.randint(key, (PARTICLES,), 0, PARTICLES))
    picked = picked.at[0].set(0)
    picked = picked.at[PARTICLES - 1].set(PARTICLES - 1)
    return picked.astype(jnp.int32)


def place_ends(entries, own_key, low, top_value):
    longest = entries.shape.index(max(entries.shape))
    spots = []
    for shift in (0, 1):
        where = [jax.random.randint(jax.random.fold_in(own_key, axis), (), 0, length) for axis, length in enumerate(entries.shape)]
        where[longest] = (where[longest] + shift) % entries.shape[longest]
        spots.append(tuple(where))
    return entries.at[spots[0]].set(low).at[spots[1]].set(top_value)


def block_scale(stream_key, shape, cuts, low, largest):
    factor_of, own = 1.0, jax.random.fold_in(stream_key, 6)
    for axis_at, shards_of in cuts:
        heights = jnp.exp(jax.random.uniform(jax.random.fold_in(own, axis_at), (shards_of,), jnp.float32, low / len(cuts), largest / len(cuts)))
        factor_of = factor_of * jnp.repeat(heights, shape[axis_at] // shards_of).reshape([-1 if axis == axis_at else 1 for axis in range(len(shape))])
    return factor_of


def normal_values(rng, shape, deviation, limit, cuts=(), kind=jnp.bfloat16):
    values = jax.random.normal(rng, shape, jnp.float32) * deviation
    if len(cuts) > 0:
        values = block_scale(rng, shape, cuts, -0.22, 0.18) * values
    return jnp.clip(values, min=-limit, max=limit).astype(kind)


def setup_inputs(seed: int = 0, part: int = 0) -> dict:
    keys = jax.random.split(jax.random.key(seed), 9)
    own_keys = jax.random.split(jax.random.fold_in(keys[8], part), 9)
    states = draw_states(jax.random.fold_in(jax.random.fold_in(keys[8], part), 71), part)
    ancestors = draw_ancestors(jax.random.fold_in(jax.random.fold_in(keys[8], part), 71), part)
    noise = normal_values(own_keys[2], (PARTICLES, TOKENS, D), 1.0, 6.0, ((0, 2), (1, 8)))
    pair = draw_pair(jax.random.fold_in(jax.random.fold_in(keys[8], part), 71), part)
    token_mask = place_ends((jax.random.randint(own_keys[4], (TOKENS,), 0, 8) < 7).astype(jnp.int32), jax.random.fold_in(own_keys[4], 1), 0, 1)
    w_qkv = normal_values(keys[5], (LAYERS, D, 3 * D), D ** -0.5, 0.21875)
    w_out = normal_values(keys[6], (LAYERS, D, D), D ** -0.5, 0.21875)
    w_pair = normal_values(keys[7], (LAYERS, C_PAIR, HEADS), 0.25, 1.5)
    return {"states": states, "ancestors": ancestors, "noise": noise, "pair": pair, "token_mask": token_mask, "w_qkv": w_qkv, "w_out": w_out, "w_pair": w_pair}


def layer_norm(stream):
    values = stream.astype(jnp.float32)
    average = lax.optimization_barrier(jnp.mean(values, axis=-1, keepdims=True))
    centred = values - average
    spread = lax.optimization_barrier(jnp.mean(centred * centred, axis=-1, keepdims=True))
    return centred * lax.rsqrt(spread + 1e-05)

def attend_one(query_one, key_one, value_one, full_bias):
    scores = jnp.einsum('ihe,jhe->hij', query_one.astype(jnp.float32), key_one.astype(jnp.float32)) + full_bias
    weights = jax.nn.softmax(scores, axis=-1).astype(jnp.bfloat16)
    return jnp.einsum('hij,jhe->ihe', weights.astype(jnp.float32), value_one.astype(jnp.float32)).astype(jnp.bfloat16)

def reference(states, ancestors, noise, pair, token_mask, w_qkv, w_out, w_pair):
    chosen = jnp.take(states, ancestors, axis=0)
    stream = (chosen.astype(jnp.float32) + 0.5 * noise.astype(jnp.float32)).astype(jnp.bfloat16)
    penalty = jnp.where(token_mask > 0, 0.0, -1000000000.0).astype(jnp.float32)
    pair_wide = pair.astype(jnp.float32)
    query_scale = HEAD_DIM ** (-0.5)
    for layer_index in range(LAYERS):
        full_bias = jnp.einsum('ijc,ch->hij', pair_wide, w_pair[layer_index].astype(jnp.float32)) + penalty[None, None, :]
        normed = layer_norm(stream).astype(jnp.bfloat16)
        projected = jnp.dot(normed.reshape(PARTICLES * TOKENS, D), w_qkv[layer_index], preferred_element_type=jnp.float32)
        projected = projected.reshape(PARTICLES, TOKENS, 3 * D)
        query = (projected[..., :D] * query_scale).astype(jnp.bfloat16).reshape(PARTICLES, TOKENS, HEADS, HEAD_DIM)
        key_rows = projected[..., D:2 * D].astype(jnp.bfloat16).reshape(PARTICLES, TOKENS, HEADS, HEAD_DIM)
        value_rows = projected[..., 2 * D:].astype(jnp.bfloat16).reshape(PARTICLES, TOKENS, HEADS, HEAD_DIM)
        attended = lax.map(lambda trio: attend_one(trio[0], trio[1], trio[2], full_bias), (query, key_rows, value_rows))
        attended = attended.reshape(PARTICLES * TOKENS, D)
        update = jnp.dot(attended, w_out[layer_index], preferred_element_type=jnp.float32).reshape(PARTICLES, TOKENS, D)
        stream = (stream.astype(jnp.float32) + update).astype(jnp.bfloat16)
    return stream
```

```python
import functools

import jax
import jax.numpy as jnp
from jax import lax
from jax.experimental import pallas as pl
from jax.experimental.pallas import tpu as pltpu
from jax.sharding import PartitionSpec as P


def layer_norm(stream):
    values = stream.astype(jnp.float32)
    average = jnp.mean(values, axis=-1, keepdims=True)
    centred = values - average
    spread = jnp.mean(centred * centred, axis=-1, keepdims=True)
    return centred * lax.rsqrt(spread + 1e-05)


def token_split_body(states, ancestors, noise, pair, token_mask, w_qkv, w_out, w_pair):
    part_count = states.shape[0]
    tok_rows = states.shape[1]
    model_width = states.shape[2]
    head_count = w_pair.shape[2]
    head_width = model_width // head_count
    layer_count = w_qkv.shape[0]
    total_keys = pair.shape[1]
    everyone = lax.all_gather(states, "dom", axis=0, tiled=True)
    chosen = jnp.take(everyone, ancestors, axis=0)
    stream = (chosen.astype(jnp.float32) + 0.5 * noise.astype(jnp.float32)).astype(jnp.bfloat16)
    penalty = jnp.where(token_mask > 0, 0.0, -1000000000.0).astype(jnp.float32)
    pair_terms = jnp.einsum("ijc,lch->lhij", pair, w_pair, preferred_element_type=jnp.float32)
    full_bias = pair_terms + penalty[None, None, None, :]
    query_scale = head_width ** (-0.5)
    for layer_index in range(layer_count):
        normed = layer_norm(stream).astype(jnp.bfloat16)
        projected = jnp.dot(
            normed.reshape(part_count * tok_rows, model_width),
            w_qkv[layer_index],
            preferred_element_type=jnp.float32,
        )
        projected = projected.reshape(part_count, tok_rows, 3 * model_width)
        query = (projected[..., :model_width] * query_scale).astype(jnp.bfloat16)
        key_tiles = projected[..., model_width : 2 * model_width].astype(jnp.bfloat16)
        value_tiles = projected[..., 2 * model_width :].astype(jnp.bfloat16)
        layer_bias = full_bias[layer_index]
        query_heads = query.reshape(part_count, tok_rows, head_count, head_width)
        all_keys, all_values = (
            lax.all_gather(key_tiles, "tok", axis=1, tiled=True),
            lax.all_gather(value_tiles, "tok", axis=1, tiled=True),
        )
        key_heads = all_keys.reshape(part_count, total_keys, head_count, head_width)
        scores = (
            jnp.einsum(
                "pihe,pjhe->phij", query_heads, key_heads, preferred_element_type=jnp.float32
            )
            + layer_bias[None]
        )
        weights = jax.nn.softmax(scores, axis=-1).astype(jnp.bfloat16)
        value_heads = all_values.reshape(part_count, total_keys, head_count, head_width)
        attended = jnp.einsum(
            "phij,pjhe->pihe", weights, value_heads, preferred_element_type=jnp.float32
        ).astype(jnp.bfloat16)
        attended = attended.reshape(part_count * tok_rows, model_width)
        update = jnp.dot(attended, w_out[layer_index], preferred_element_type=jnp.float32)
        update = update.reshape(part_count, tok_rows, model_width)
        stream = (stream.astype(jnp.float32) + update).astype(jnp.bfloat16)
    return stream


MESH = pl.DeviceIdType.MESH
LANES = 128


def particle_kernel(
    peers,
    head_count,
    ancestors,
    states,
    noise,
    pair,
    token_mask,
    w_pair,
    w_qkv_hbm,
    w_out_hbm,
    result,
    everyone,
    outgoing,
    stream_in,
    bias,
    bias_rows,
    qkv,
    finished,
    w_qkv,
    w_out,
    weight_sem,
    state_sem,
    stream_send,
    stream_recv,
    bias_send,
    bias_recv,
    relay_send,
    relay_recv,
    out_send,
    out_recv,
):
    group = lax.axis_index("groups")
    me = lax.axis_index("tok")
    core = lax.axis_index("dom")
    sibling = (group, me, 1 - core)
    part_count, tok_rows, width = states.shape
    layer_count = w_qkv.shape[0]
    tokens = peers * tok_rows
    head_width = width // head_count
    half_heads = head_count // 2

    def ahead(step):
        return lax.rem(me + step, peers)

    def behind(step):
        return lax.rem(me + peers - step, peers)

    def remote(source, target, send, recv, device):
        return pltpu.make_async_remote_copy(
            src_ref=source,
            dst_ref=target,
            send_sem=send,
            recv_sem=recv,
            device_id=device,
            device_id_type=MESH,
        )

    weight_copies = []
    for layer in range(layer_count):
        weight_copies.append(
            (
                pltpu.make_async_copy(w_qkv_hbm.at[layer], w_qkv.at[layer], weight_sem.at[layer, 0]),
                pltpu.make_async_copy(w_out_hbm.at[layer], w_out.at[layer], weight_sem.at[layer, 1]),
            )
        )
    for qkv_copy, out_copy in weight_copies:
        qkv_copy.start()
        out_copy.start()

    barrier = pltpu.get_barrier_semaphore()
    pl.semaphore_signal(barrier, inc=1, device_id=sibling, device_id_type=MESH)
    for step in range(1, peers):
        pl.semaphore_signal(
            barrier, inc=1, device_id=(group, ahead(step), core), device_id_type=MESH
        )
    pl.semaphore_wait(barrier, peers)

    mine = pl.ds(core * part_count, part_count)
    state_copy = remote(states, everyone.at[mine], state_sem.at[0], state_sem.at[1], sibling)
    state_copy.start()
    everyone[mine] = states[...]

    penalty = jnp.where(token_mask[...] > 0, 0.0, -1000000000.0).astype(jnp.float32)
    w_rows = jnp.concatenate(
        [w_pair[layer].astype(jnp.float32).T for layer in range(layer_count)], axis=0
    ).astype(jnp.bfloat16)
    for row in range(tok_rows):
        full = (
            lax.dot_general(
                w_rows, pair[row], (((1,), (1,)), ((), ())), preferred_element_type=jnp.float32
            )
            + penalty
        )
        bias_rows[:, row, :] = full - jnp.max(full, axis=-1, keepdims=True)
    for layer in range(layer_count):
        bias[layer, me] = bias_rows[pl.ds(layer * head_count, head_count)].astype(jnp.bfloat16)

    state_copy.wait()

    def moved(particle):
        chosen = everyone[ancestors[particle]].astype(jnp.float32)
        return (chosen + 0.5 * noise[particle].astype(jnp.float32)).astype(jnp.bfloat16)

    stream_copies = []
    for step in range(1, peers):
        target = ahead(step)
        outgoing[step] = moved(target)
        copy = remote(
            outgoing.at[step],
            stream_in.at[me],
            stream_send.at[step],
            stream_recv.at[step],
            (group, target, core),
        )
        copy.start()
        stream_copies.append(copy)
    stream_in[me] = moved(me)

    my_heads = pl.ds(core * half_heads, half_heads)
    bias_copies = []
    for layer in range(layer_count):
        layer_copies = []
        for step in range(1, peers):
            copy = remote(
                bias.at[layer, me, my_heads],
                bias.at[layer, me, my_heads],
                bias_send.at[layer, step],
                bias_recv.at[layer, step],
                (group, ahead(step), core),
            )
            copy.start()
            layer_copies.append(copy)
        bias_copies.append(layer_copies)

    def relay(layer):
        copies = []
        for step in range(1, peers):
            bias_copies[layer][step - 1].wait_recv()
            block = bias.at[layer, behind(step), my_heads]
            copy = remote(
                block, block, relay_send.at[layer, step], relay_recv.at[layer, step], sibling
            )
            copy.start()
            copies.append(copy)
        return copies

    for copy in stream_copies:
        copy.wait_recv()
    stream = stream_in[...].reshape(tokens, width)

    lanes = lax.broadcasted_iota(jnp.int32, (1, LANES), 1)
    relays = []
    for layer in range(layer_count):
        normed = layer_norm(stream).astype(jnp.bfloat16)
        weight_copies[layer][0].wait()
        for block in range(3):
            columns = pl.ds(block * width, width)
            projected = jnp.dot(
                normed, w_qkv[layer, :, columns], preferred_element_type=jnp.float32
            )
            if block == 0:
                projected = projected * head_width ** (-0.5)
            qkv[:, columns] = projected.astype(jnp.bfloat16)
        if layer == 0:
            relays.append(relay(0))
        for copy in relays[layer]:
            copy.wait_recv()
        tiles = [None] * (width // LANES)
        for head in range(head_count):
            low, high = head * head_width, (head + 1) * head_width
            first, last = low // LANES, (high + LANES - 1) // LANES
            masks = [
                (lanes >= low - tile * LANES) & (lanes < high - tile * LANES)
                for tile in range(first, last)
            ]
            start, size = first * LANES, (last - first) * LANES
            keep = jnp.concatenate(
                [jnp.where(mask, 1.0, 0.0).astype(jnp.bfloat16) for mask in masks], axis=1
            )
            scores = lax.dot_general(
                qkv[:, pl.ds(start, size)] * keep,
                qkv[:, pl.ds(width + start, size)],
                (((1,), (1,)), ((), ())),
                preferred_element_type=jnp.float32,
            )
            scores = scores + bias[layer, :, head].reshape(tokens, tokens).astype(jnp.float32)
            raised = jnp.exp(scores - jnp.max(scores, axis=-1, keepdims=True))
            weights = (raised / jnp.sum(raised, axis=-1, keepdims=True)).astype(jnp.bfloat16)
            part = jnp.dot(
                weights,
                qkv[:, pl.ds(2 * width + start, size)],
                preferred_element_type=jnp.float32,
            )
            for place, mask in enumerate(masks):
                piece = part[:, place * LANES : (place + 1) * LANES]
                held = tiles[first + place]
                tiles[first + place] = piece if held is None else jnp.where(mask, piece, held)
        attended = jnp.concatenate([tile.astype(jnp.bfloat16) for tile in tiles], axis=1)
        if layer + 1 < layer_count:
            relays.append(relay(layer + 1))
        weight_copies[layer][1].wait()
        update = jnp.dot(attended, w_out[layer], preferred_element_type=jnp.float32)
        stream = (stream.astype(jnp.float32) + update).astype(jnp.bfloat16)

    finished[...] = stream.reshape(peers, tok_rows, width)
    out_copies = []
    for step in range(1, peers):
        target = ahead(step)
        copy = remote(
            finished.at[target],
            result.at[me],
            out_send.at[step],
            out_recv.at[step],
            (group, target, core),
        )
        copy.start()
        out_copies.append(copy)
    result[me] = finished[me]
    for copies in [stream_copies] + bias_copies + relays:
        for copy in copies:
            copy.wait_send()
    for copy in out_copies:
        copy.wait()


def particle_body(peers, states, ancestors, noise, pair, token_mask, w_qkv, w_out, w_pair):
    part_count, tok_rows, width = states.shape
    layer_count, _, head_count = w_pair.shape
    tokens = peers * tok_rows
    vmem = pl.BlockSpec(memory_space=pltpu.VMEM)
    smem = pl.BlockSpec(memory_space=pltpu.SMEM)
    anywhere = pl.BlockSpec(memory_space=pl.ANY)
    dma = pltpu.SemaphoreType.DMA
    per_peer, per_layer = dma((peers,)), dma((layer_count, peers))
    return pl.pallas_call(
        functools.partial(particle_kernel, peers, head_count),
        out_shape=jax.ShapeDtypeStruct(states.shape, states.dtype),
        in_specs=[smem, vmem, vmem, vmem, vmem, vmem, anywhere, anywhere],
        out_specs=vmem,
        scratch_shapes=[
            pltpu.VMEM((2 * part_count, tok_rows, width), jnp.bfloat16),
            pltpu.VMEM((peers, tok_rows, width), jnp.bfloat16),
            pltpu.VMEM((peers, tok_rows, width), jnp.bfloat16),
            pltpu.VMEM((layer_count, peers, head_count, tok_rows, tokens), jnp.bfloat16),
            pltpu.VMEM((layer_count * head_count, tok_rows, tokens), jnp.float32),
            pltpu.VMEM((tokens, 3 * width), jnp.bfloat16),
            pltpu.VMEM((peers, tok_rows, width), jnp.bfloat16),
            pltpu.VMEM(w_qkv.shape, w_qkv.dtype),
            pltpu.VMEM(w_out.shape, w_out.dtype),
            dma((layer_count, 2)),
            dma((2,)),
            per_peer,
            per_peer,
            per_layer,
            per_layer,
            per_layer,
            per_layer,
            per_peer,
            per_peer,
        ],
        compiler_params=pltpu.CompilerParams(
            collective_id=0, has_side_effects=True, vmem_limit_bytes=40 * 1024 * 1024
        ),
        name="particle_layers",
    )(ancestors, states, noise, pair, token_mask.reshape(1, tokens), w_pair, w_qkv, w_out)


def body(peers, states, ancestors, noise, pair, token_mask, w_qkv, w_out, w_pair):
    part_count, tok_rows, width = states.shape
    one_each = part_count == peers and tok_rows % 16 == 0 and peers * tok_rows == LANES
    inner = functools.partial(particle_body, peers) if one_each else token_split_body
    return inner(states, ancestors, noise, pair, token_mask, w_qkv, w_out, w_pair)


def solution(mesh):
    placed = (
        P(("groups", "dom"), "tok", None),
        P(("groups", "dom")),
        P(("groups", "dom"), "tok", None),
        P(("groups", "tok"), None, None),
        P("groups"),
        P(),
        P(),
        P(),
    )
    return jax.shard_map(
        functools.partial(body, mesh.shape["tok"]),
        mesh=mesh,
        in_specs=placed,
        out_specs=P(("groups", "dom"), "tok", None),
        check_vma=False,
    )
```

```python
import functools

import jax
import jax.numpy as jnp
from jax import lax
from jax.experimental import pallas as pl
from jax.experimental.pallas import tpu as pltpu
from jax.sharding import PartitionSpec as P


def layer_norm(stream):
    values = stream.astype(jnp.float32)
    average = jnp.mean(values, axis=-1, keepdims=True)
    centred = values - average
    spread = jnp.mean(centred * centred, axis=-1, keepdims=True)
    return centred * lax.rsqrt(spread + 1e-05)


def token_split_body(states, ancestors, noise, pair, token_mask, w_qkv, w_out, w_pair):
    part_count = states.shape[0]
    tok_rows = states.shape[1]
    model_width = states.shape[2]
    head_count = w_pair.shape[2]
    head_width = model_width // head_count
    layer_count = w_qkv.shape[0]
    total_keys = pair.shape[1]
    everyone = lax.all_gather(states, "dom", axis=0, tiled=True)
    chosen = jnp.take(everyone, ancestors, axis=0)
    stream = (chosen.astype(jnp.float32) + 0.5 * noise.astype(jnp.float32)).astype(jnp.bfloat16)
    penalty = jnp.where(token_mask > 0, 0.0, -1000000000.0).astype(jnp.float32)
    pair_terms = jnp.einsum("ijc,lch->lhij", pair, w_pair, preferred_element_type=jnp.float32)
    full_bias = pair_terms + penalty[None, None, None, :]
    query_scale = head_width ** (-0.5)
    for layer_index in range(layer_count):
        normed = layer_norm(stream).astype(jnp.bfloat16)
        projected = jnp.dot(
            normed.reshape(part_count * tok_rows, model_width),
            w_qkv[layer_index],
            preferred_element_type=jnp.float32,
        )
        projected = projected.reshape(part_count, tok_rows, 3 * model_width)
        query = (projected[..., :model_width] * query_scale).astype(jnp.bfloat16)
        key_tiles = projected[..., model_width : 2 * model_width].astype(jnp.bfloat16)
        value_tiles = projected[..., 2 * model_width :].astype(jnp.bfloat16)
        layer_bias = full_bias[layer_index]
        query_heads = query.reshape(part_count, tok_rows, head_count, head_width)
        all_keys, all_values = (
            lax.all_gather(key_tiles, "tok", axis=1, tiled=True),
            lax.all_gather(value_tiles, "tok", axis=1, tiled=True),
        )
        key_heads = all_keys.reshape(part_count, total_keys, head_count, head_width)
        scores = (
            jnp.einsum(
                "pihe,pjhe->phij", query_heads, key_heads, preferred_element_type=jnp.float32
            )
            + layer_bias[None]
        )
        weights = jax.nn.softmax(scores, axis=-1).astype(jnp.bfloat16)
        value_heads = all_values.reshape(part_count, total_keys, head_count, head_width)
        attended = jnp.einsum(
            "phij,pjhe->pihe", weights, value_heads, preferred_element_type=jnp.float32
        ).astype(jnp.bfloat16)
        attended = attended.reshape(part_count * tok_rows, model_width)
        update = jnp.dot(attended, w_out[layer_index], preferred_element_type=jnp.float32)
        update = update.reshape(part_count, tok_rows, model_width)
        stream = (stream.astype(jnp.float32) + update).astype(jnp.bfloat16)
    return stream


MESH = pl.DeviceIdType.MESH
LANES = 128


def particle_kernel(
    peers,
    head_count,
    ancestors_hbm,
    states,
    noise_hbm,
    pair_hbm,
    mask_hbm,
    w_pair_hbm,
    w_qkv_hbm,
    w_out_hbm,
    result,
    ancestors,
    noise,
    pair,
    token_mask,
    w_pair,
    everyone,
    outgoing,
    stream_in,
    bias,
    bias_rows,
    qkv,
    finished,
    w_qkv,
    w_out,
    load_sem,
    weight_sem,
    state_sem,
    stream_send,
    stream_recv,
    bias_send,
    bias_recv,
    relay_send,
    relay_recv,
    out_send,
    out_recv,
):
    group = lax.axis_index("groups")
    me = lax.axis_index("tok")
    core = lax.axis_index("dom")
    sibling = (group, me, 1 - core)
    part_count, tok_rows, width = states.shape
    layer_count = w_qkv.shape[0]
    tokens = peers * tok_rows
    head_width = width // head_count
    half_heads = head_count // 2

    def ahead(step):
        return lax.rem(me + step, peers)

    def behind(step):
        return lax.rem(me + peers - step, peers)

    def remote(source, target, send, recv, device):
        return pltpu.make_async_remote_copy(
            src_ref=source,
            dst_ref=target,
            send_sem=send,
            recv_sem=recv,
            device_id=device,
            device_id_type=MESH,
        )

    weight_copies = []
    for layer in range(layer_count):
        weight_copies.append(
            (
                pltpu.make_async_copy(w_qkv_hbm.at[layer], w_qkv.at[layer], weight_sem.at[layer, 0]),
                pltpu.make_async_copy(w_out_hbm.at[layer], w_out.at[layer], weight_sem.at[layer, 1]),
            )
        )
    mine = pl.ds(core * part_count, part_count)
    loads = []
    for place, (source, target) in enumerate(
        (
            (pair_hbm, pair),
            (w_pair_hbm, w_pair),
            (mask_hbm, token_mask),
            (ancestors_hbm, ancestors),
            (states, everyone.at[mine]),
            (noise_hbm, noise),
        )
    ):
        loads.append(pltpu.make_async_copy(source, target, load_sem.at[place]))
        loads[-1].start()

    barrier = pltpu.get_barrier_semaphore()
    pl.semaphore_signal(barrier, inc=1, device_id=sibling, device_id_type=MESH)
    for step in range(1, peers):
        pl.semaphore_signal(
            barrier, inc=1, device_id=(group, ahead(step), core), device_id_type=MESH
        )
    pl.semaphore_wait(barrier, peers)

    state_copy = remote(states, everyone.at[mine], state_sem.at[0], state_sem.at[1], sibling)
    state_copy.start()
    for qkv_copy, out_copy in weight_copies:
        qkv_copy.start()
        out_copy.start()

    for load in loads[:3]:
        load.wait()
    penalty = jnp.where(token_mask[...] > 0, 0.0, -1000000000.0).astype(jnp.float32)
    w_rows = w_pair[...].reshape(layer_count * head_count, w_pair.shape[2])
    for row in range(tok_rows):
        full = (
            lax.dot_general(
                w_rows, pair[row], (((1,), (1,)), ((), ())), preferred_element_type=jnp.float32
            )
            + penalty
        )
        bias_rows[:, row, :] = full - jnp.max(full, axis=-1, keepdims=True)
    for layer in range(layer_count):
        bias[layer, me] = bias_rows[pl.ds(layer * head_count, head_count)].astype(jnp.bfloat16)

    for load in loads[3:]:
        load.wait()
    state_copy.wait()

    def moved(particle):
        chosen = everyone[ancestors[particle]].astype(jnp.float32)
        return (chosen + 0.5 * noise[particle].astype(jnp.float32)).astype(jnp.bfloat16)

    stream_copies = []
    for step in range(1, peers):
        target = ahead(step)
        outgoing[step] = moved(target)
        copy = remote(
            outgoing.at[step],
            stream_in.at[me],
            stream_send.at[step],
            stream_recv.at[step],
            (group, target, core),
        )
        copy.start()
        stream_copies.append(copy)
    stream_in[me] = moved(me)

    my_heads = pl.ds(core * half_heads, half_heads)
    pairs = peers // 2
    partner = me + 1 - 2 * lax.rem(me, 2)
    bias_copies = []

    def send_bias(layer, slot, owner, target):
        block = bias.at[layer, owner, my_heads]
        copy = remote(
            block,
            block,
            bias_send.at[layer, slot],
            bias_recv.at[layer, slot],
            (group, target, core),
        )
        copy.start()
        bias_copies.append(copy)
        return copy

    def spread(layer):
        copies = [send_bias(layer, 0, me, partner)]
        for step in range(1, pairs):
            copies.append(send_bias(layer, step, me, ahead(2 * step)))
        return copies

    def hand_over(layer, slot, owner):
        block = bias.at[layer, owner, my_heads]
        copy = remote(
            block, block, relay_send.at[layer, slot], relay_recv.at[layer, slot], sibling
        )
        copy.start()
        return copy

    def relay_own_parity(layer, copies):
        handed = []
        for step in range(1, pairs):
            copies[step].wait_recv()
            copies.append(send_bias(layer, pairs - 1 + step, behind(2 * step), partner))
            handed.append(hand_over(layer, step, behind(2 * step)))
        copies[0].wait_recv()
        handed.append(hand_over(layer, 0, partner))
        return handed

    def relay_partner(layer, copies):
        handed = []
        for step in range(1, pairs):
            slot = pairs - 1 + step
            copies[slot].wait_recv()
            owner = lax.rem(partner + peers - 2 * step, peers)
            handed.append(hand_over(layer, slot, owner))
        return handed

    spreads = [spread(0)]
    relays = []

    for copy in stream_copies:
        copy.wait_recv()
    stream = stream_in[...].reshape(tokens, width)

    ones = jnp.ones((tokens, LANES), jnp.bfloat16)
    lanes = lax.broadcasted_iota(jnp.int32, (1, LANES), 1)
    for layer in range(layer_count):
        normed = layer_norm(stream).astype(jnp.bfloat16)
        weight_copies[layer][0].wait()
        for block in range(3):
            columns = pl.ds(block * width, width)
            projected = jnp.dot(
                normed, w_qkv[layer, :, columns], preferred_element_type=jnp.float32
            )
            if block == 0:
                projected = projected * head_width ** (-0.5)
            qkv[:, columns] = projected.astype(jnp.bfloat16)
        if layer == 0:
            relays.append(relay_own_parity(0, spreads[0]))
            relays[0] += relay_partner(0, spreads[0])
        for copy in relays[layer]:
            copy.wait_recv()
        if layer + 1 < layer_count:
            spreads.append(spread(layer + 1))
        tiles = [None] * (width // LANES)
        for head in range(head_count):
            low, high = head * head_width, (head + 1) * head_width
            first, last = low // LANES, (high + LANES - 1) // LANES
            masks = [
                (lanes >= low - tile * LANES) & (lanes < high - tile * LANES)
                for tile in range(first, last)
            ]
            start, size = first * LANES, (last - first) * LANES
            keep = jnp.concatenate(
                [jnp.where(mask, 1.0, 0.0).astype(jnp.bfloat16) for mask in masks], axis=1
            )
            scores = lax.dot_general(
                qkv[:, pl.ds(start, size)] * keep,
                qkv[:, pl.ds(width + start, size)],
                (((1,), (1,)), ((), ())),
                preferred_element_type=jnp.float32,
            )
            scores = scores + bias[layer, :, head].reshape(tokens, tokens).astype(jnp.float32)
            raised = jnp.exp(scores - jnp.max(scores, axis=-1, keepdims=True)).astype(jnp.bfloat16)
            values = jnp.concatenate([qkv[:, pl.ds(2 * width + start, size)], ones], axis=1)
            part = jnp.dot(raised, values, preferred_element_type=jnp.float32)
            inverse = 1.0 / part[:, size:]
            for place, mask in enumerate(masks):
                piece = part[:, place * LANES : (place + 1) * LANES] * inverse
                held = tiles[first + place]
                tiles[first + place] = piece if held is None else jnp.where(mask, piece, held)
        attended = jnp.concatenate([tile.astype(jnp.bfloat16) for tile in tiles], axis=1)
        if layer + 1 < layer_count:
            relays.append(relay_own_parity(layer + 1, spreads[layer + 1]))
        weight_copies[layer][1].wait()
        update = jnp.dot(attended, w_out[layer], preferred_element_type=jnp.float32)
        stream = (stream.astype(jnp.float32) + update).astype(jnp.bfloat16)
        if layer + 1 < layer_count:
            relays[layer + 1] += relay_partner(layer + 1, spreads[layer + 1])

    finished[...] = stream.reshape(peers, tok_rows, width)
    out_copies = []
    for step in range(1, peers):
        target = ahead(step)
        copy = remote(
            finished.at[target],
            result.at[me],
            out_send.at[step],
            out_recv.at[step],
            (group, target, core),
        )
        copy.start()
        out_copies.append(copy)
    result[me] = finished[me]
    for copies in [stream_copies, bias_copies] + relays:
        for copy in copies:
            copy.wait_send()
    for copy in out_copies:
        copy.wait()


def particle_body(peers, states, ancestors, noise, pair, token_mask, w_qkv, w_out, w_pair):
    part_count, tok_rows, width = states.shape
    layer_count, _, head_count = w_pair.shape
    tokens = peers * tok_rows
    vmem = pl.BlockSpec(memory_space=pltpu.VMEM)
    hbm = pl.BlockSpec(memory_space=pltpu.HBM)
    dma = pltpu.SemaphoreType.DMA
    per_peer, per_layer = dma((peers,)), dma((layer_count, peers))
    return pl.pallas_call(
        functools.partial(particle_kernel, peers, head_count),
        out_shape=jax.ShapeDtypeStruct(states.shape, states.dtype),
        in_specs=[hbm] * 8,
        out_specs=vmem,
        scratch_shapes=[
            pltpu.SMEM(ancestors.shape, ancestors.dtype),
            pltpu.VMEM(noise.shape, noise.dtype),
            pltpu.VMEM(pair.shape, pair.dtype),
            pltpu.VMEM((1, tokens), token_mask.dtype),
            pltpu.VMEM((layer_count, head_count, w_pair.shape[1]), w_pair.dtype),
            pltpu.VMEM((2 * part_count, tok_rows, width), jnp.bfloat16),
            pltpu.VMEM((peers, tok_rows, width), jnp.bfloat16),
            pltpu.VMEM((peers, tok_rows, width), jnp.bfloat16),
            pltpu.VMEM((layer_count, peers, head_count, tok_rows, tokens), jnp.bfloat16),
            pltpu.VMEM((layer_count * head_count, tok_rows, tokens), jnp.float32),
            pltpu.VMEM((tokens, 3 * width), jnp.bfloat16),
            pltpu.VMEM((peers, tok_rows, width), jnp.bfloat16),
            pltpu.VMEM(w_qkv.shape, w_qkv.dtype),
            pltpu.VMEM(w_out.shape, w_out.dtype),
            dma((6,)),
            dma((layer_count, 2)),
            dma((2,)),
            per_peer,
            per_peer,
            per_layer,
            per_layer,
            per_layer,
            per_layer,
            per_peer,
            per_peer,
        ],
        compiler_params=pltpu.CompilerParams(
            collective_id=0, has_side_effects=True, vmem_limit_bytes=63 * 1024 * 1024
        ),
        name="particle_layers",
    )(
        ancestors,
        states,
        noise,
        pair,
        token_mask.reshape(1, tokens),
        jnp.transpose(w_pair, (0, 2, 1)),
        w_qkv,
        w_out,
    )


def body(peers, states, ancestors, noise, pair, token_mask, w_qkv, w_out, w_pair):
    part_count, tok_rows, width = states.shape
    one_each = part_count == peers and peers % 2 == 0 and tok_rows % 16 == 0 and peers * tok_rows == LANES
    inner = functools.partial(particle_body, peers) if one_each else token_split_body
    return inner(states, ancestors, noise, pair, token_mask, w_qkv, w_out, w_pair)


def solution(mesh):
    placed = (
        P(("groups", "dom"), "tok", None),
        P(("groups", "dom")),
        P(("groups", "dom"), "tok", None),
        P(("groups", "tok"), None, None),
        P("groups"),
        P(),
        P(),
        P(),
    )
    return jax.shard_map(
        functools.partial(body, mesh.shape["tok"]),
        mesh=mesh,
        in_specs=placed,
        out_specs=P(("groups", "dom"), "tok", None),
        check_vma=False,
    )
```

```python
import functools

import jax
import jax.numpy as jnp
from jax import lax
from jax.experimental import pallas as pl
from jax.experimental.pallas import tpu as pltpu
from jax.sharding import PartitionSpec as P


def layer_norm(stream):
    values = stream.astype(jnp.float32)
    average = jnp.mean(values, axis=-1, keepdims=True)
    centred = values - average
    spread = jnp.mean(centred * centred, axis=-1, keepdims=True)
    return centred * lax.rsqrt(spread + 1e-05)


def token_split_body(states, ancestors, noise, pair, token_mask, w_qkv, w_out, w_pair):
    part_count = states.shape[0]
    tok_rows = states.shape[1]
    model_width = states.shape[2]
    head_count = w_pair.shape[2]
    head_width = model_width // head_count
    layer_count = w_qkv.shape[0]
    total_keys = pair.shape[1]
    everyone = lax.all_gather(states, "dom", axis=0, tiled=True)
    chosen = jnp.take(everyone, ancestors, axis=0)
    stream = (chosen.astype(jnp.float32) + 0.5 * noise.astype(jnp.float32)).astype(jnp.bfloat16)
    penalty = jnp.where(token_mask > 0, 0.0, -1000000000.0).astype(jnp.float32)
    pair_terms = jnp.einsum("ijc,lch->lhij", pair, w_pair, preferred_element_type=jnp.float32)
    full_bias = pair_terms + penalty[None, None, None, :]
    query_scale = head_width ** (-0.5)
    for layer_index in range(layer_count):
        normed = layer_norm(stream).astype(jnp.bfloat16)
        projected = jnp.dot(
            normed.reshape(part_count * tok_rows, model_width),
            w_qkv[layer_index],
            preferred_element_type=jnp.float32,
        )
        projected = projected.reshape(part_count, tok_rows, 3 * model_width)
        query = (projected[..., :model_width] * query_scale).astype(jnp.bfloat16)
        key_tiles = projected[..., model_width : 2 * model_width].astype(jnp.bfloat16)
        value_tiles = projected[..., 2 * model_width :].astype(jnp.bfloat16)
        layer_bias = full_bias[layer_index]
        query_heads = query.reshape(part_count, tok_rows, head_count, head_width)
        all_keys, all_values = (
            lax.all_gather(key_tiles, "tok", axis=1, tiled=True),
            lax.all_gather(value_tiles, "tok", axis=1, tiled=True),
        )
        key_heads = all_keys.reshape(part_count, total_keys, head_count, head_width)
        scores = (
            jnp.einsum(
                "pihe,pjhe->phij", query_heads, key_heads, preferred_element_type=jnp.float32
            )
            + layer_bias[None]
        )
        weights = jax.nn.softmax(scores, axis=-1).astype(jnp.bfloat16)
        value_heads = all_values.reshape(part_count, total_keys, head_count, head_width)
        attended = jnp.einsum(
            "phij,pjhe->pihe", weights, value_heads, preferred_element_type=jnp.float32
        ).astype(jnp.bfloat16)
        attended = attended.reshape(part_count * tok_rows, model_width)
        update = jnp.dot(attended, w_out[layer_index], preferred_element_type=jnp.float32)
        update = update.reshape(part_count, tok_rows, model_width)
        stream = (stream.astype(jnp.float32) + update).astype(jnp.bfloat16)
    return stream


MESH = pl.DeviceIdType.MESH
LANES = 128


def particle_kernel(
    peers,
    head_count,
    ancestors_hbm,
    states,
    noise_hbm,
    pair_hbm,
    mask_hbm,
    w_pair_hbm,
    w_qkv_hbm,
    w_out_hbm,
    result,
    ancestors,
    noise,
    pair,
    token_mask,
    w_pair,
    everyone,
    outgoing,
    stream_in,
    bias,
    bias_rows,
    qkv,
    score_rows,
    raised,
    finished,
    w_qkv,
    w_out,
    load_sem,
    weight_sem,
    state_sem,
    stream_send,
    stream_recv,
    bias_send,
    bias_recv,
    relay_send,
    relay_recv,
    out_send,
    out_recv,
):
    group = lax.axis_index("groups")
    me = lax.axis_index("tok")
    core = lax.axis_index("dom")
    sibling = (group, me, 1 - core)
    part_count, tok_rows, width = states.shape
    layer_count = w_qkv.shape[0]
    tokens = peers * tok_rows
    head_width = width // head_count
    half_heads = head_count // 2

    def ahead(step):
        return lax.rem(me + step, peers)

    def behind(step):
        return lax.rem(me + peers - step, peers)

    def remote(source, target, send, recv, device):
        return pltpu.make_async_remote_copy(
            src_ref=source,
            dst_ref=target,
            send_sem=send,
            recv_sem=recv,
            device_id=device,
            device_id_type=MESH,
        )

    weight_copies = []
    for layer in range(layer_count):
        weight_copies.append(
            (
                pltpu.make_async_copy(w_qkv_hbm.at[layer], w_qkv.at[layer], weight_sem.at[layer, 0]),
                pltpu.make_async_copy(w_out_hbm.at[layer], w_out.at[layer], weight_sem.at[layer, 1]),
            )
        )
    mine = pl.ds(core * part_count, part_count)
    loads = []
    for place, (source, target) in enumerate(
        (
            (pair_hbm, pair),
            (w_pair_hbm, w_pair),
            (mask_hbm, token_mask),
            (ancestors_hbm, ancestors),
            (states, everyone.at[mine]),
            (noise_hbm, noise),
        )
    ):
        loads.append(pltpu.make_async_copy(source, target, load_sem.at[place]))
        loads[-1].start()

    barrier = pltpu.get_barrier_semaphore()
    pl.semaphore_signal(barrier, inc=1, device_id=sibling, device_id_type=MESH)
    for step in range(1, peers):
        pl.semaphore_signal(
            barrier, inc=1, device_id=(group, ahead(step), core), device_id_type=MESH
        )
    pl.semaphore_wait(barrier, peers)

    state_copy = remote(states, everyone.at[mine], state_sem.at[0], state_sem.at[1], sibling)
    state_copy.start()
    for qkv_copy, out_copy in weight_copies:
        qkv_copy.start()
        out_copy.start()

    for load in loads[:3]:
        load.wait()
    penalty = jnp.where(token_mask[...] > 0, 0.0, -1000000000.0).astype(jnp.float32)
    w_rows = w_pair[...].reshape(layer_count * head_count, w_pair.shape[2])
    for row in range(tok_rows):
        full = (
            lax.dot_general(
                w_rows, pair[row], (((1,), (1,)), ((), ())), preferred_element_type=jnp.float32
            )
            + penalty
        )
        bias_rows[:, row, :] = full - jnp.max(full, axis=-1, keepdims=True)
    for layer in range(layer_count):
        bias[layer, me] = bias_rows[pl.ds(layer * head_count, head_count)].astype(jnp.bfloat16)

    for load in loads[3:]:
        load.wait()
    state_copy.wait()

    def moved(particle):
        chosen = everyone[ancestors[particle]].astype(jnp.float32)
        return (chosen + 0.5 * noise[particle].astype(jnp.float32)).astype(jnp.bfloat16)

    stream_copies = []
    for step in range(1, peers):
        target = ahead(step)
        outgoing[step] = moved(target)
        copy = remote(
            outgoing.at[step],
            stream_in.at[me],
            stream_send.at[step],
            stream_recv.at[step],
            (group, target, core),
        )
        copy.start()
        stream_copies.append(copy)
    stream_in[me] = moved(me)

    my_heads = pl.ds(core * half_heads, half_heads)
    pairs = peers // 2
    partner = me + 1 - 2 * lax.rem(me, 2)
    bias_copies = []

    def send_bias(layer, slot, owner, target):
        block = bias.at[layer, owner, my_heads]
        copy = remote(
            block,
            block,
            bias_send.at[layer, slot],
            bias_recv.at[layer, slot],
            (group, target, core),
        )
        copy.start()
        bias_copies.append(copy)
        return copy

    def spread(layer):
        copies = [send_bias(layer, 0, me, partner)]
        for step in range(1, pairs):
            copies.append(send_bias(layer, step, me, ahead(2 * step)))
        return copies

    def hand_over(layer, slot, owner):
        block = bias.at[layer, owner, my_heads]
        copy = remote(
            block, block, relay_send.at[layer, slot], relay_recv.at[layer, slot], sibling
        )
        copy.start()
        return copy

    def relay_own_parity(layer, copies):
        handed = []
        for step in range(1, pairs):
            copies[step].wait_recv()
            copies.append(send_bias(layer, pairs - 1 + step, behind(2 * step), partner))
            handed.append(hand_over(layer, step, behind(2 * step)))
        copies[0].wait_recv()
        handed.append(hand_over(layer, 0, partner))
        return handed

    def relay_partner(layer, copies):
        handed = []
        for step in range(1, pairs):
            slot = pairs - 1 + step
            copies[slot].wait_recv()
            owner = lax.rem(partner + peers - 2 * step, peers)
            handed.append(hand_over(layer, slot, owner))
        return handed

    spreads = [spread(0)]
    relays = []

    for copy in stream_copies:
        copy.wait_recv()
    stream = stream_in[...].reshape(tokens, width)

    def head_lanes(head, start, size):
        lanes = lax.broadcasted_iota(jnp.int32, (1, size), 1) + start
        inside = (lanes >= head * head_width) & (lanes < (head + 1) * head_width)
        return jnp.where(inside, 1.0, 0.0).astype(jnp.bfloat16)

    windows = []
    for head in range(head_count):
        if windows and (head + 1) * head_width <= windows[-1][0] + 2 * LANES:
            windows[-1][1].append(head)
        else:
            start = head * head_width // LANES * LANES
            windows.append((min(start, width - 2 * LANES), [head]))

    for layer in range(layer_count):
        normed = layer_norm(stream).astype(jnp.bfloat16)
        weight_copies[layer][0].wait()
        for block in range(3):
            columns = pl.ds(block * width, width)
            projected = jnp.dot(
                normed, w_qkv[layer, :, columns], preferred_element_type=jnp.float32
            )
            if block == 0:
                projected = projected * head_width ** (-0.5)
            qkv[:, columns] = projected.astype(jnp.bfloat16)
        if layer == 0:
            relays.append(relay_own_parity(0, spreads[0]))
        for start, heads in windows:
            query = qkv[:, pl.ds(start, 2 * LANES)]
            score_rows[pl.ds(heads[0] * tokens, len(heads) * tokens)] = lax.dot_general(
                jnp.concatenate(
                    [query * head_lanes(head, start, 2 * LANES) for head in heads], axis=0
                ),
                qkv[:, pl.ds(width + start, 2 * LANES)],
                (((1,), (1,)), ((), ())),
                preferred_element_type=jnp.float32,
            )
        if layer == 0:
            relays[0] += relay_partner(0, spreads[0])
        for copy in relays[layer]:
            copy.wait_recv()
        if layer + 1 < layer_count:
            spreads.append(spread(layer + 1))
        tiles = []
        ready = 0
        for tile in range(width // LANES):
            start = tile * LANES
            first = start // head_width
            last = (start + LANES + head_width - 1) // head_width
            for head in range(ready, last):
                scores = score_rows[pl.ds(head * tokens, tokens)] + bias[layer, :, head].reshape(
                    tokens, tokens
                ).astype(jnp.float32)
                largest = jnp.max(scores, axis=-1, keepdims=True)
                raised[:, pl.ds(head * tokens, tokens)] = jnp.exp(scores - largest).astype(
                    jnp.bfloat16
                )
            ready = last
            value = qkv[:, pl.ds(2 * width + start, LANES)]
            masks = [
                jnp.broadcast_to(head_lanes(head, start, LANES), (tokens, LANES))
                for head in range(first, last)
            ]
            sides = jnp.concatenate(
                [jnp.concatenate([value * mask, mask], axis=1) for mask in masks], axis=0
            )
            part = jnp.dot(
                raised[:, pl.ds(first * tokens, (last - first) * tokens)],
                sides,
                preferred_element_type=jnp.float32,
            )
            tiles.append((part[:, :LANES] / part[:, LANES:]).astype(jnp.bfloat16))
        attended = jnp.concatenate(tiles, axis=1)
        if layer + 1 < layer_count:
            relays.append(relay_own_parity(layer + 1, spreads[layer + 1]))
        weight_copies[layer][1].wait()
        update = jnp.dot(attended, w_out[layer], preferred_element_type=jnp.float32)
        stream = (stream.astype(jnp.float32) + update).astype(jnp.bfloat16)
        if layer + 1 < layer_count:
            relays[layer + 1] += relay_partner(layer + 1, spreads[layer + 1])

    finished[...] = stream.reshape(peers, tok_rows, width)
    out_copies = []
    for step in range(1, peers):
        target = ahead(step)
        copy = remote(
            finished.at[target],
            result.at[me],
            out_send.at[step],
            out_recv.at[step],
            (group, target, core),
        )
        copy.start()
        out_copies.append(copy)
    kept = pltpu.make_async_copy(finished.at[me], result.at[me], load_sem.at[6])
    kept.start()
    kept.wait()
    for copies in [stream_copies, bias_copies] + relays:
        for copy in copies:
            copy.wait_send()
    for copy in out_copies:
        copy.wait()


def particle_body(peers, states, ancestors, noise, pair, token_mask, w_qkv, w_out, w_pair):
    part_count, tok_rows, width = states.shape
    layer_count, _, head_count = w_pair.shape
    tokens = peers * tok_rows
    hbm = pl.BlockSpec(memory_space=pltpu.HBM)
    dma = pltpu.SemaphoreType.DMA
    per_peer, per_layer = dma((peers,)), dma((layer_count, peers))
    return pl.pallas_call(
        functools.partial(particle_kernel, peers, head_count),
        out_shape=jax.ShapeDtypeStruct(states.shape, states.dtype),
        in_specs=[hbm] * 8,
        out_specs=hbm,
        scratch_shapes=[
            pltpu.SMEM(ancestors.shape, ancestors.dtype),
            pltpu.VMEM(noise.shape, noise.dtype),
            pltpu.VMEM(pair.shape, pair.dtype),
            pltpu.VMEM((1, tokens), token_mask.dtype),
            pltpu.VMEM((layer_count, head_count, w_pair.shape[1]), w_pair.dtype),
            pltpu.VMEM((2 * part_count, tok_rows, width), jnp.bfloat16),
            pltpu.VMEM((peers, tok_rows, width), jnp.bfloat16),
            pltpu.VMEM((peers, tok_rows, width), jnp.bfloat16),
            pltpu.VMEM((layer_count, peers, head_count, tok_rows, tokens), jnp.bfloat16),
            pltpu.VMEM((layer_count * head_count, tok_rows, tokens), jnp.float32),
            pltpu.VMEM((tokens, 3 * width), jnp.bfloat16),
            pltpu.VMEM((head_count * tokens, tokens), jnp.float32),
            pltpu.VMEM((tokens, head_count * tokens), jnp.bfloat16),
            pltpu.VMEM((peers, tok_rows, width), jnp.bfloat16),
            pltpu.VMEM(w_qkv.shape, w_qkv.dtype),
            pltpu.VMEM(w_out.shape, w_out.dtype),
            dma((7,)),
            dma((layer_count, 2)),
            dma((2,)),
            per_peer,
            per_peer,
            per_layer,
            per_layer,
            per_layer,
            per_layer,
            per_peer,
            per_peer,
        ],
        compiler_params=pltpu.CompilerParams(
            collective_id=0, has_side_effects=True, vmem_limit_bytes=63 * 1024 * 1024
        ),
        name="particle_layers",
    )(
        ancestors,
        states,
        noise,
        pair,
        token_mask.reshape(1, tokens),
        jnp.transpose(w_pair, (0, 2, 1)),
        w_qkv,
        w_out,
    )


def body(peers, states, ancestors, noise, pair, token_mask, w_qkv, w_out, w_pair):
    part_count, tok_rows, width = states.shape
    one_each = part_count == peers and peers % 2 == 0 and tok_rows % 16 == 0 and peers * tok_rows == LANES and width % LANES == 0
    inner = functools.partial(particle_body, peers) if one_each else token_split_body
    return inner(states, ancestors, noise, pair, token_mask, w_qkv, w_out, w_pair)


def solution(mesh):
    placed = (
        P(("groups", "dom"), "tok", None),
        P(("groups", "dom")),
        P(("groups", "dom"), "tok", None),
        P(("groups", "tok"), None, None),
        P("groups"),
        P(),
        P(),
        P(),
    )
    return jax.shard_map(
        functools.partial(body, mesh.shape["tok"]),
        mesh=mesh,
        in_specs=placed,
        out_specs=P(("groups", "dom"), "tok", None),
        check_vma=False,
    )
```

```python
import functools

import jax
import jax.numpy as jnp
from jax import lax
from jax.experimental import pallas as pl
from jax.experimental.pallas import tpu as pltpu
from jax.sharding import PartitionSpec as P


def layer_norm(stream):
    values = stream.astype(jnp.float32)
    average = jnp.mean(values, axis=-1, keepdims=True)
    centred = values - average
    spread = jnp.mean(centred * centred, axis=-1, keepdims=True)
    return centred * lax.rsqrt(spread + 1e-05)


def token_split_body(states, ancestors, noise, pair, token_mask, w_qkv, w_out, w_pair):
    part_count = states.shape[0]
    tok_rows = states.shape[1]
    model_width = states.shape[2]
    head_count = w_pair.shape[2]
    head_width = model_width // head_count
    layer_count = w_qkv.shape[0]
    total_keys = pair.shape[1]
    everyone = lax.all_gather(states, "dom", axis=0, tiled=True)
    chosen = jnp.take(everyone, ancestors, axis=0)
    stream = (chosen.astype(jnp.float32) + 0.5 * noise.astype(jnp.float32)).astype(jnp.bfloat16)
    penalty = jnp.where(token_mask > 0, 0.0, -1000000000.0).astype(jnp.float32)
    pair_terms = jnp.einsum("ijc,lch->lhij", pair, w_pair, preferred_element_type=jnp.float32)
    full_bias = pair_terms + penalty[None, None, None, :]
    query_scale = head_width ** (-0.5)
    for layer_index in range(layer_count):
        normed = layer_norm(stream).astype(jnp.bfloat16)
        projected = jnp.dot(
            normed.reshape(part_count * tok_rows, model_width),
            w_qkv[layer_index],
            preferred_element_type=jnp.float32,
        )
        projected = projected.reshape(part_count, tok_rows, 3 * model_width)
        query = (projected[..., :model_width] * query_scale).astype(jnp.bfloat16)
        key_tiles = projected[..., model_width : 2 * model_width].astype(jnp.bfloat16)
        value_tiles = projected[..., 2 * model_width :].astype(jnp.bfloat16)
        layer_bias = full_bias[layer_index]
        query_heads = query.reshape(part_count, tok_rows, head_count, head_width)
        all_keys, all_values = (
            lax.all_gather(key_tiles, "tok", axis=1, tiled=True),
            lax.all_gather(value_tiles, "tok", axis=1, tiled=True),
        )
        key_heads = all_keys.reshape(part_count, total_keys, head_count, head_width)
        scores = (
            jnp.einsum(
                "pihe,pjhe->phij", query_heads, key_heads, preferred_element_type=jnp.float32
            )
            + layer_bias[None]
        )
        weights = jax.nn.softmax(scores, axis=-1).astype(jnp.bfloat16)
        value_heads = all_values.reshape(part_count, total_keys, head_count, head_width)
        attended = jnp.einsum(
            "phij,pjhe->pihe", weights, value_heads, preferred_element_type=jnp.float32
        ).astype(jnp.bfloat16)
        attended = attended.reshape(part_count * tok_rows, model_width)
        update = jnp.dot(attended, w_out[layer_index], preferred_element_type=jnp.float32)
        update = update.reshape(part_count, tok_rows, model_width)
        stream = (stream.astype(jnp.float32) + update).astype(jnp.bfloat16)
    return stream


MESH = pl.DeviceIdType.MESH
LANES = 128


def particle_kernel(
    peers,
    head_count,
    ancestors_hbm,
    states,
    noise_hbm,
    pair_hbm,
    mask_hbm,
    w_pair_hbm,
    w_qkv_hbm,
    w_out_hbm,
    result,
    ancestors,
    noise,
    pair,
    token_mask,
    w_pair,
    everyone,
    outgoing,
    stream_in,
    bias,
    bias_rows,
    qkv,
    score_rows,
    raised,
    finished,
    w_qkv,
    w_out,
    load_sem,
    weight_sem,
    state_sem,
    stream_send,
    stream_recv,
    bias_send,
    bias_recv,
    relay_send,
    relay_recv,
    out_send,
    out_recv,
):
    group = lax.axis_index("groups")
    me = lax.axis_index("tok")
    core = lax.axis_index("dom")
    sibling = (group, me, 1 - core)
    part_count, tok_rows, width = states.shape
    layer_count = w_qkv.shape[0]
    tokens = peers * tok_rows
    head_width = width // head_count
    half_heads = head_count // 2

    def ahead(step):
        return lax.rem(me + step, peers)

    def behind(step):
        return lax.rem(me + peers - step, peers)

    half = peers // 2
    side, place_in_half = me // half, lax.rem(me, half)
    far = [
        (half + step, (1 - side) * half + lax.rem(place_in_half + step, half))
        for step in range(half)
    ]
    near = [
        (step, side * half + lax.rem(place_in_half + step, half)) for step in range(1, half)
    ]
    exchanges = far + near

    def remote(source, target, send, recv, device):
        return pltpu.make_async_remote_copy(
            src_ref=source,
            dst_ref=target,
            send_sem=send,
            recv_sem=recv,
            device_id=device,
            device_id_type=MESH,
        )

    weight_copies = []
    for layer in range(layer_count):
        weight_copies.append(
            (
                pltpu.make_async_copy(w_qkv_hbm.at[layer], w_qkv.at[layer], weight_sem.at[layer, 0]),
                pltpu.make_async_copy(w_out_hbm.at[layer], w_out.at[layer], weight_sem.at[layer, 1]),
            )
        )
    mine = pl.ds(core * part_count, part_count)
    loads = []
    for place, (source, target) in enumerate(
        (
            (ancestors_hbm, ancestors),
            (states, everyone.at[mine]),
            (noise_hbm, noise),
            (pair_hbm, pair),
            (w_pair_hbm, w_pair),
            (mask_hbm, token_mask),
        )
    ):
        loads.append(pltpu.make_async_copy(source, target, load_sem.at[place]))
        loads[-1].start()

    barrier = pltpu.get_barrier_semaphore()
    pl.semaphore_signal(barrier, inc=1, device_id=sibling, device_id_type=MESH)
    for step in range(1, peers):
        pl.semaphore_signal(
            barrier, inc=1, device_id=(group, ahead(step), core), device_id_type=MESH
        )
    pl.semaphore_wait(barrier, peers)

    state_copy = remote(states, everyone.at[mine], state_sem.at[0], state_sem.at[1], sibling)
    state_copy.start()
    for qkv_copy, out_copy in weight_copies:
        qkv_copy.start()
        out_copy.start()

    for load in loads[:3]:
        load.wait()
    state_copy.wait()

    def moved(particle):
        chosen = everyone[ancestors[particle]].astype(jnp.float32)
        return (chosen + 0.5 * noise[particle].astype(jnp.float32)).astype(jnp.bfloat16)

    stream_copies = []
    for step, target in exchanges:
        outgoing[step] = moved(target)
        copy = remote(
            outgoing.at[step],
            stream_in.at[me],
            stream_send.at[step],
            stream_recv.at[step],
            (group, target, core),
        )
        copy.start()
        stream_copies.append(copy)
    stream_in[me] = moved(me)

    for load in loads[3:]:
        load.wait()
    penalty = jnp.where(token_mask[...] > 0, 0.0, -1000000000.0).astype(jnp.float32)
    w_rows = w_pair[...].reshape(layer_count * head_count, w_pair.shape[2])
    for row in range(tok_rows):
        full = (
            lax.dot_general(
                w_rows, pair[row], (((1,), (1,)), ((), ())), preferred_element_type=jnp.float32
            )
            + penalty
        )
        bias_rows[:, row, :] = full - jnp.max(full, axis=-1, keepdims=True)
    for layer in range(layer_count):
        bias[layer, me] = bias_rows[pl.ds(layer * head_count, head_count)].astype(jnp.bfloat16)

    my_heads = pl.ds(core * half_heads, half_heads)
    pairs = peers // 2
    partner = me + 1 - 2 * lax.rem(me, 2)
    bias_copies = []

    def send_bias(layer, slot, owner, target):
        block = bias.at[layer, owner, my_heads]
        copy = remote(
            block,
            block,
            bias_send.at[layer, slot],
            bias_recv.at[layer, slot],
            (group, target, core),
        )
        copy.start()
        bias_copies.append(copy)
        return copy

    def spread(layer):
        copies = [send_bias(layer, 0, me, partner)]
        for step in range(1, pairs):
            copies.append(send_bias(layer, step, me, ahead(2 * step)))
        return copies

    def hand_over(layer, slot, owner):
        block = bias.at[layer, owner, my_heads]
        copy = remote(
            block, block, relay_send.at[layer, slot], relay_recv.at[layer, slot], sibling
        )
        copy.start()
        return copy

    def relay_own_parity(layer, copies):
        handed = []
        for step in range(1, pairs):
            copies[step].wait_recv()
            copies.append(send_bias(layer, pairs - 1 + step, behind(2 * step), partner))
            handed.append(hand_over(layer, step, behind(2 * step)))
        copies[0].wait_recv()
        handed.append(hand_over(layer, 0, partner))
        return handed

    def relay_partner(layer, copies):
        handed = []
        for step in range(1, pairs):
            slot = pairs - 1 + step
            copies[slot].wait_recv()
            owner = lax.rem(partner + peers - 2 * step, peers)
            handed.append(hand_over(layer, slot, owner))
        return handed

    spreads = [spread(0)]
    relays = []

    for copy in stream_copies:
        copy.wait_recv()

    def head_lanes(head, start, size):
        lanes = lax.broadcasted_iota(jnp.int32, (1, size), 1) + start
        inside = (lanes >= head * head_width) & (lanes < (head + 1) * head_width)
        return jnp.where(inside, 1.0, 0.0).astype(jnp.bfloat16)

    def attend(layer, first_block, blocks, kept_rows):
        rows = blocks * tok_rows
        tiles = []
        ready = 0
        for tile in range(width // LANES):
            start = tile * LANES
            first = start // head_width
            last = (start + LANES + head_width - 1) // head_width
            for head in range(ready, last):
                first_score = pl.multiple_of(head * tokens + first_block * tok_rows, tok_rows)
                bias_block = bias[layer, pl.ds(first_block, blocks), head]
                scores = score_rows[pl.ds(first_score, rows)] + bias_block.reshape(
                    rows, tokens
                ).astype(jnp.float32)
                largest = jnp.max(scores, axis=-1, keepdims=True)
                raised[kept_rows, pl.ds(head * tokens, tokens)] = jnp.exp(scores - largest).astype(
                    jnp.bfloat16
                )
            ready = last
            value = qkv[:, pl.ds(2 * width + start, LANES)]
            masks = [
                jnp.broadcast_to(head_lanes(head, start, LANES), (tokens, LANES))
                for head in range(first, last)
            ]
            sides = jnp.concatenate(
                [jnp.concatenate([value * mask, mask], axis=1) for mask in masks], axis=0
            )
            part = jnp.dot(
                raised[kept_rows, pl.ds(first * tokens, (last - first) * tokens)],
                sides,
                preferred_element_type=jnp.float32,
            )
            tiles.append((part[:, :LANES] / part[:, LANES:]).astype(jnp.bfloat16))
        return jnp.concatenate(tiles, axis=1)

    def project(layer, first_block, blocks, attended):
        update = jnp.dot(attended, w_out[layer], preferred_element_type=jnp.float32)
        old = stream_in[pl.ds(first_block, blocks)].astype(jnp.float32)
        return (old + update.reshape(old.shape)).astype(jnp.bfloat16)

    windows = []
    for head in range(head_count):
        if windows and (head + 1) * head_width <= windows[-1][0] + 2 * LANES:
            windows[-1][1].append(head)
        else:
            start = head * head_width // LANES * LANES
            windows.append((min(start, width - 2 * LANES), [head]))

    for layer in range(layer_count):
        stream = stream_in[...].reshape(tokens, width)
        normed = layer_norm(stream).astype(jnp.bfloat16)
        weight_copies[layer][0].wait()
        for block in range(3):
            columns = pl.ds(block * width, width)
            projected = jnp.dot(
                normed, w_qkv[layer, :, columns], preferred_element_type=jnp.float32
            )
            if block == 0:
                projected = projected * head_width ** (-0.5)
            qkv[:, columns] = projected.astype(jnp.bfloat16)
        if layer == 0:
            relays.append(relay_own_parity(0, spreads[0]))
        for start, heads in windows:
            query = qkv[:, pl.ds(start, 2 * LANES)]
            score_rows[pl.ds(heads[0] * tokens, len(heads) * tokens)] = lax.dot_general(
                jnp.concatenate(
                    [query * head_lanes(head, start, 2 * LANES) for head in heads], axis=0
                ),
                qkv[:, pl.ds(width + start, 2 * LANES)],
                (((1,), (1,)), ((), ())),
                preferred_element_type=jnp.float32,
            )
        if layer == 0:
            relays[0] += relay_partner(0, spreads[0])
        for copy in relays[layer]:
            copy.wait_recv()
        if layer + 1 < layer_count:
            spreads.append(spread(layer + 1))
        if layer + 1 < layer_count:
            attended = attend(layer, 0, peers, pl.ds(0, tokens))
            relays.append(relay_own_parity(layer + 1, spreads[layer + 1]))
            weight_copies[layer][1].wait()
            stream_in[...] = project(layer, 0, peers, attended)
            relays[layer + 1] += relay_partner(layer + 1, spreads[layer + 1])

    last = layer_count - 1
    weight_copies[last][1].wait()
    out_copies = []
    for turn, (owner, exchange) in enumerate(((1 - side, far), (side, near))):
        first_block = owner * half
        kept_rows = pl.ds(turn * half * tok_rows, half * tok_rows)
        attended = attend(last, first_block, half, kept_rows)
        finished[pl.ds(first_block, half)] = project(last, first_block, half, attended)
        for slot, target in exchange:
            copy = remote(
                finished.at[target],
                result.at[me],
                out_send.at[slot],
                out_recv.at[slot],
                (group, target, core),
            )
            copy.start()
            out_copies.append(copy)
    kept = pltpu.make_async_copy(finished.at[me], result.at[me], load_sem.at[6])
    kept.start()
    kept.wait()
    for copies in [stream_copies, bias_copies] + relays:
        for copy in copies:
            copy.wait_send()
    for copy in out_copies:
        copy.wait()


def particle_body(peers, states, ancestors, noise, pair, token_mask, w_qkv, w_out, w_pair):
    part_count, tok_rows, width = states.shape
    layer_count, _, head_count = w_pair.shape
    tokens = peers * tok_rows
    hbm = pl.BlockSpec(memory_space=pltpu.HBM)
    dma = pltpu.SemaphoreType.DMA
    per_peer, per_layer = dma((peers,)), dma((layer_count, peers))
    return pl.pallas_call(
        functools.partial(particle_kernel, peers, head_count),
        out_shape=jax.ShapeDtypeStruct(states.shape, states.dtype),
        in_specs=[hbm] * 8,
        out_specs=hbm,
        scratch_shapes=[
            pltpu.SMEM(ancestors.shape, ancestors.dtype),
            pltpu.VMEM(noise.shape, noise.dtype),
            pltpu.VMEM(pair.shape, pair.dtype),
            pltpu.VMEM((1, tokens), token_mask.dtype),
            pltpu.VMEM((layer_count, head_count, w_pair.shape[1]), w_pair.dtype),
            pltpu.VMEM((2 * part_count, tok_rows, width), jnp.bfloat16),
            pltpu.VMEM((peers, tok_rows, width), jnp.bfloat16),
            pltpu.VMEM((peers, tok_rows, width), jnp.bfloat16),
            pltpu.VMEM((layer_count, peers, head_count, tok_rows, tokens), jnp.bfloat16),
            pltpu.VMEM((layer_count * head_count, tok_rows, tokens), jnp.float32),
            pltpu.VMEM((tokens, 3 * width), jnp.bfloat16),
            pltpu.VMEM((head_count * tokens, tokens), jnp.float32),
            pltpu.VMEM((tokens, head_count * tokens), jnp.bfloat16),
            pltpu.VMEM((peers, tok_rows, width), jnp.bfloat16),
            pltpu.VMEM(w_qkv.shape, w_qkv.dtype),
            pltpu.VMEM(w_out.shape, w_out.dtype),
            dma((7,)),
            dma((layer_count, 2)),
            dma((2,)),
            per_peer,
            per_peer,
            per_layer,
            per_layer,
            per_layer,
            per_layer,
            per_peer,
            per_peer,
        ],
        compiler_params=pltpu.CompilerParams(
            collective_id=0, has_side_effects=True, vmem_limit_bytes=63 * 1024 * 1024
        ),
        name="particle_layers",
    )(
        ancestors,
        states,
        noise,
        pair,
        token_mask.reshape(1, tokens),
        jnp.transpose(w_pair, (0, 2, 1)),
        w_qkv,
        w_out,
    )


def body(peers, states, ancestors, noise, pair, token_mask, w_qkv, w_out, w_pair):
    part_count, tok_rows, width = states.shape
    one_each = part_count == peers and peers % 2 == 0 and tok_rows % 16 == 0 and peers * tok_rows == LANES and width % LANES == 0
    inner = functools.partial(particle_body, peers) if one_each else token_split_body
    return inner(states, ancestors, noise, pair, token_mask, w_qkv, w_out, w_pair)


def solution(mesh):
    placed = (
        P(("groups", "dom"), "tok", None),
        P(("groups", "dom")),
        P(("groups", "dom"), "tok", None),
        P(("groups", "tok"), None, None),
        P("groups"),
        P(),
        P(),
        P(),
    )
    return jax.shard_map(
        functools.partial(body, mesh.shape["tok"]),
        mesh=mesh,
        in_specs=placed,
        out_specs=P(("groups", "dom"), "tok", None),
        check_vma=False,
    )
```

```python
import functools

import jax
import jax.numpy as jnp
from jax import lax
from jax.experimental import pallas as pl
from jax.experimental.pallas import tpu as pltpu
from jax.sharding import PartitionSpec as P


def layer_norm(stream):
    values = stream.astype(jnp.float32)
    average = jnp.mean(values, axis=-1, keepdims=True)
    centred = values - average
    spread = jnp.mean(centred * centred, axis=-1, keepdims=True)
    return centred * lax.rsqrt(spread + 1e-05)


def token_split_body(states, ancestors, noise, pair, token_mask, w_qkv, w_out, w_pair):
    part_count = states.shape[0]
    tok_rows = states.shape[1]
    model_width = states.shape[2]
    head_count = w_pair.shape[2]
    head_width = model_width // head_count
    layer_count = w_qkv.shape[0]
    total_keys = pair.shape[1]
    everyone = lax.all_gather(states, "dom", axis=0, tiled=True)
    chosen = jnp.take(everyone, ancestors, axis=0)
    stream = (chosen.astype(jnp.float32) + 0.5 * noise.astype(jnp.float32)).astype(jnp.bfloat16)
    penalty = jnp.where(token_mask > 0, 0.0, -1000000000.0).astype(jnp.float32)
    pair_terms = jnp.einsum("ijc,lch->lhij", pair, w_pair, preferred_element_type=jnp.float32)
    full_bias = pair_terms + penalty[None, None, None, :]
    query_scale = head_width ** (-0.5)
    for layer_index in range(layer_count):
        normed = layer_norm(stream).astype(jnp.bfloat16)
        projected = jnp.dot(
            normed.reshape(part_count * tok_rows, model_width),
            w_qkv[layer_index],
            preferred_element_type=jnp.float32,
        )
        projected = projected.reshape(part_count, tok_rows, 3 * model_width)
        query = (projected[..., :model_width] * query_scale).astype(jnp.bfloat16)
        key_tiles = projected[..., model_width : 2 * model_width].astype(jnp.bfloat16)
        value_tiles = projected[..., 2 * model_width :].astype(jnp.bfloat16)
        layer_bias = full_bias[layer_index]
        query_heads = query.reshape(part_count, tok_rows, head_count, head_width)
        all_keys, all_values = (
            lax.all_gather(key_tiles, "tok", axis=1, tiled=True),
            lax.all_gather(value_tiles, "tok", axis=1, tiled=True),
        )
        key_heads = all_keys.reshape(part_count, total_keys, head_count, head_width)
        scores = (
            jnp.einsum(
                "pihe,pjhe->phij", query_heads, key_heads, preferred_element_type=jnp.float32
            )
            + layer_bias[None]
        )
        weights = jax.nn.softmax(scores, axis=-1).astype(jnp.bfloat16)
        value_heads = all_values.reshape(part_count, total_keys, head_count, head_width)
        attended = jnp.einsum(
            "phij,pjhe->pihe", weights, value_heads, preferred_element_type=jnp.float32
        ).astype(jnp.bfloat16)
        attended = attended.reshape(part_count * tok_rows, model_width)
        update = jnp.dot(attended, w_out[layer_index], preferred_element_type=jnp.float32)
        update = update.reshape(part_count, tok_rows, model_width)
        stream = (stream.astype(jnp.float32) + update).astype(jnp.bfloat16)
    return stream


MESH = pl.DeviceIdType.MESH
LANES = 128


def particle_kernel(
    peers,
    head_count,
    ancestors_hbm,
    states,
    noise_hbm,
    pair_hbm,
    mask_hbm,
    w_pair_hbm,
    w_qkv_hbm,
    w_out_hbm,
    result,
    ancestors,
    noise,
    pair,
    token_mask,
    w_pair,
    everyone,
    outgoing,
    stream_in,
    bias,
    bias_rows,
    qkv,
    score_rows,
    raised,
    finished,
    w_qkv,
    w_out,
    load_sem,
    weight_sem,
    state_sem,
    stream_send,
    stream_recv,
    bias_send,
    bias_recv,
    relay_send,
    relay_recv,
    out_send,
    out_recv,
):
    group = lax.axis_index("groups")
    me = lax.axis_index("tok")
    core = lax.axis_index("dom")
    sibling = (group, me, 1 - core)
    part_count, tok_rows, width = states.shape
    layer_count = w_qkv.shape[0]
    tokens = peers * tok_rows
    head_width = width // head_count
    half_heads = head_count // 2

    def ahead(step):
        return lax.rem(me + step, peers)

    def behind(step):
        return lax.rem(me + peers - step, peers)

    half = peers // 2
    side, place_in_half = me // half, lax.rem(me, half)
    far = [
        (half + step, (1 - side) * half + lax.rem(place_in_half + step, half))
        for step in range(half)
    ]
    near = [
        (step, side * half + lax.rem(place_in_half + step, half)) for step in range(1, half)
    ]
    exchanges = far + near

    def remote(source, target, send, recv, device):
        return pltpu.make_async_remote_copy(
            src_ref=source,
            dst_ref=target,
            send_sem=send,
            recv_sem=recv,
            device_id=device,
            device_id_type=MESH,
        )

    weight_copies = []
    for layer in range(layer_count):
        weight_copies.append(
            (
                pltpu.make_async_copy(w_qkv_hbm.at[layer], w_qkv.at[layer], weight_sem.at[layer, 0]),
                pltpu.make_async_copy(w_out_hbm.at[layer], w_out.at[layer], weight_sem.at[layer, 1]),
            )
        )
    mine = pl.ds(core * part_count, part_count)
    loads = []
    for place, (source, target) in enumerate(
        (
            (pair_hbm, pair),
            (w_pair_hbm, w_pair),
            (mask_hbm, token_mask),
            (ancestors_hbm, ancestors),
            (states, everyone.at[mine]),
            (noise_hbm, noise),
        )
    ):
        loads.append(pltpu.make_async_copy(source, target, load_sem.at[place]))
        loads[-1].start()

    barrier = pltpu.get_barrier_semaphore()
    pl.semaphore_signal(barrier, inc=1, device_id=sibling, device_id_type=MESH)
    for step in range(1, peers):
        pl.semaphore_signal(
            barrier, inc=1, device_id=(group, ahead(step), core), device_id_type=MESH
        )

    for load in loads[:3]:
        load.wait()
    penalty = jnp.where(token_mask[...] > 0, 0.0, -1000000000.0).astype(jnp.float32)
    w_rows = w_pair[...].reshape(layer_count * head_count, w_pair.shape[2])
    pair_terms = lax.dot_general(
        w_rows,
        pair[...].reshape(tok_rows * tokens, pair.shape[2]),
        (((1,), (1,)), ((), ())),
        preferred_element_type=jnp.float32,
    )
    for row in range(tok_rows):
        full = pair_terms[:, row * tokens : (row + 1) * tokens] + penalty
        bias_rows[:, row, :] = full - jnp.max(full, axis=-1, keepdims=True)
    for layer in range(layer_count):
        bias[layer, me] = bias_rows[pl.ds(layer * head_count, head_count)].astype(jnp.bfloat16)

    pl.semaphore_wait(barrier, peers)

    state_copy = remote(states, everyone.at[mine], state_sem.at[0], state_sem.at[1], sibling)
    state_copy.start()
    my_heads = pl.ds(core * half_heads, half_heads)
    pairs = peers // 2
    partner = me + 1 - 2 * lax.rem(me, 2)
    bias_copies = []

    def send_bias(layer, slot, owner, target):
        block = bias.at[layer, owner, my_heads]
        copy = remote(
            block,
            block,
            bias_send.at[layer, slot],
            bias_recv.at[layer, slot],
            (group, target, core),
        )
        copy.start()
        bias_copies.append(copy)
        return copy

    def spread(layer):
        copies = [send_bias(layer, 0, me, partner)]
        for step in range(1, pairs):
            copies.append(send_bias(layer, step, me, ahead(2 * step)))
        return copies

    def hand_over(layer, slot, owner):
        block = bias.at[layer, owner, my_heads]
        copy = remote(
            block, block, relay_send.at[layer, slot], relay_recv.at[layer, slot], sibling
        )
        copy.start()
        return copy

    def relay_own_parity(layer, copies):
        handed = []
        for step in range(1, pairs):
            copies[step].wait_recv()
            copies.append(send_bias(layer, pairs - 1 + step, behind(2 * step), partner))
            handed.append(hand_over(layer, step, behind(2 * step)))
        copies[0].wait_recv()
        handed.append(hand_over(layer, 0, partner))
        return handed

    def relay_partner(layer, copies):
        handed = []
        for step in range(1, pairs):
            slot = pairs - 1 + step
            copies[slot].wait_recv()
            owner = lax.rem(partner + peers - 2 * step, peers)
            handed.append(hand_over(layer, slot, owner))
        return handed

    spreads = [spread(0)]
    relays = []
    for qkv_copy, out_copy in weight_copies:
        qkv_copy.start()
        out_copy.start()

    for load in loads[3:]:
        load.wait()
    state_copy.wait()

    def moved(particle):
        chosen = everyone[ancestors[particle]].astype(jnp.float32)
        return (chosen + 0.5 * noise[particle].astype(jnp.float32)).astype(jnp.bfloat16)

    stream_copies = []
    for step, target in exchanges:
        outgoing[step] = moved(target)
        copy = remote(
            outgoing.at[step],
            stream_in.at[me],
            stream_send.at[step],
            stream_recv.at[step],
            (group, target, core),
        )
        copy.start()
        stream_copies.append(copy)
    stream_in[me] = moved(me)

    relays.append(relay_own_parity(0, spreads[0]))
    relays[0] += relay_partner(0, spreads[0])

    for copy in stream_copies:
        copy.wait_recv()

    def head_lanes(head, start, size):
        lanes = lax.broadcasted_iota(jnp.int32, (1, size), 1) + start
        inside = (lanes >= head * head_width) & (lanes < (head + 1) * head_width)
        return jnp.where(inside, 1.0, 0.0).astype(jnp.bfloat16)

    def attend(layer, first_block, blocks, kept_rows):
        rows = blocks * tok_rows
        tiles = []
        ready = 0
        for tile in range(width // LANES):
            start = tile * LANES
            first = start // head_width
            last = (start + LANES + head_width - 1) // head_width
            for head in range(ready, last):
                first_score = pl.multiple_of(head * tokens + first_block * tok_rows, tok_rows)
                bias_block = bias[layer, pl.ds(first_block, blocks), head]
                scores = score_rows[pl.ds(first_score, rows)] + bias_block.reshape(
                    rows, tokens
                ).astype(jnp.float32)
                largest = jnp.max(scores, axis=-1, keepdims=True)
                raised[kept_rows, pl.ds(head * tokens, tokens)] = jnp.exp(scores - largest).astype(
                    jnp.bfloat16
                )
            ready = last
            value = qkv[:, pl.ds(2 * width + start, LANES)]
            masks = [
                jnp.broadcast_to(head_lanes(head, start, LANES), (tokens, LANES))
                for head in range(first, last)
            ]
            sides = jnp.concatenate(
                [jnp.concatenate([value * mask, mask], axis=1) for mask in masks], axis=0
            )
            part = jnp.dot(
                raised[kept_rows, pl.ds(first * tokens, (last - first) * tokens)],
                sides,
                preferred_element_type=jnp.float32,
            )
            tiles.append((part[:, :LANES] / part[:, LANES:]).astype(jnp.bfloat16))
        return jnp.concatenate(tiles, axis=1)

    def project(layer, first_block, blocks, attended):
        update = jnp.dot(attended, w_out[layer], preferred_element_type=jnp.float32)
        old = stream_in[pl.ds(first_block, blocks)].astype(jnp.float32)
        return (old + update.reshape(old.shape)).astype(jnp.bfloat16)

    windows = []
    for head in range(head_count):
        if windows and (head + 1) * head_width <= windows[-1][0] + 2 * LANES:
            windows[-1][1].append(head)
        else:
            start = head * head_width // LANES * LANES
            windows.append((min(start, width - 2 * LANES), [head]))

    for layer in range(layer_count):
        stream = stream_in[...].reshape(tokens, width)
        normed = layer_norm(stream).astype(jnp.bfloat16)
        weight_copies[layer][0].wait()
        for block in range(3):
            columns = pl.ds(block * width, width)
            projected = jnp.dot(
                normed, w_qkv[layer, :, columns], preferred_element_type=jnp.float32
            )
            if block == 0:
                projected = projected * head_width ** (-0.5)
            qkv[:, columns] = projected.astype(jnp.bfloat16)
        for start, heads in windows:
            query = qkv[:, pl.ds(start, 2 * LANES)]
            score_rows[pl.ds(heads[0] * tokens, len(heads) * tokens)] = lax.dot_general(
                jnp.concatenate(
                    [query * head_lanes(head, start, 2 * LANES) for head in heads], axis=0
                ),
                qkv[:, pl.ds(width + start, 2 * LANES)],
                (((1,), (1,)), ((), ())),
                preferred_element_type=jnp.float32,
            )
        for copy in relays[layer]:
            copy.wait_recv()
        if layer + 1 < layer_count:
            spreads.append(spread(layer + 1))
        if layer + 1 < layer_count:
            attended = attend(layer, 0, peers, pl.ds(0, tokens))
            relays.append(relay_own_parity(layer + 1, spreads[layer + 1]))
            weight_copies[layer][1].wait()
            stream_in[...] = project(layer, 0, peers, attended)
            relays[layer + 1] += relay_partner(layer + 1, spreads[layer + 1])

    last = layer_count - 1
    weight_copies[last][1].wait()
    out_copies = []
    for turn, (owner, exchange) in enumerate(((1 - side, far), (side, near))):
        first_block = owner * half
        kept_rows = pl.ds(turn * half * tok_rows, half * tok_rows)
        attended = attend(last, first_block, half, kept_rows)
        finished[pl.ds(first_block, half)] = project(last, first_block, half, attended)
        for slot, target in exchange:
            copy = remote(
                finished.at[target],
                result.at[me],
                out_send.at[slot],
                out_recv.at[slot],
                (group, target, core),
            )
            copy.start()
            out_copies.append(copy)
    kept = pltpu.make_async_copy(finished.at[me], result.at[me], load_sem.at[6])
    kept.start()
    kept.wait()
    for copies in [stream_copies, bias_copies] + relays:
        for copy in copies:
            copy.wait_send()
    for copy in out_copies:
        copy.wait()


def particle_body(peers, states, ancestors, noise, pair, token_mask, w_qkv, w_out, w_pair):
    part_count, tok_rows, width = states.shape
    layer_count, _, head_count = w_pair.shape
    tokens = peers * tok_rows
    hbm = pl.BlockSpec(memory_space=pltpu.HBM)
    dma = pltpu.SemaphoreType.DMA
    per_peer, per_layer = dma((peers,)), dma((layer_count, peers))
    return pl.pallas_call(
        functools.partial(particle_kernel, peers, head_count),
        out_shape=jax.ShapeDtypeStruct(states.shape, states.dtype),
        in_specs=[hbm] * 8,
        out_specs=hbm,
        scratch_shapes=[
            pltpu.SMEM(ancestors.shape, ancestors.dtype),
            pltpu.VMEM(noise.shape, noise.dtype),
            pltpu.VMEM(pair.shape, pair.dtype),
            pltpu.VMEM((1, tokens), token_mask.dtype),
            pltpu.VMEM((layer_count, head_count, w_pair.shape[1]), w_pair.dtype),
            pltpu.VMEM((2 * part_count, tok_rows, width), jnp.bfloat16),
            pltpu.VMEM((peers, tok_rows, width), jnp.bfloat16),
            pltpu.VMEM((peers, tok_rows, width), jnp.bfloat16),
            pltpu.VMEM((layer_count, peers, head_count, tok_rows, tokens), jnp.bfloat16),
            pltpu.VMEM((layer_count * head_count, tok_rows, tokens), jnp.float32),
            pltpu.VMEM((tokens, 3 * width), jnp.bfloat16),
            pltpu.VMEM((head_count * tokens, tokens), jnp.float32),
            pltpu.VMEM((tokens, head_count * tokens), jnp.bfloat16),
            pltpu.VMEM((peers, tok_rows, width), jnp.bfloat16),
            pltpu.VMEM(w_qkv.shape, w_qkv.dtype),
            pltpu.VMEM(w_out.shape, w_out.dtype),
            dma((7,)),
            dma((layer_count, 2)),
            dma((2,)),
            per_peer,
            per_peer,
            per_layer,
            per_layer,
            per_layer,
            per_layer,
            per_peer,
            per_peer,
        ],
        compiler_params=pltpu.CompilerParams(
            collective_id=0, has_side_effects=True, vmem_limit_bytes=63 * 1024 * 1024
        ),
        name="particle_layers",
    )(
        ancestors,
        states,
        noise,
        pair,
        token_mask.reshape(1, tokens),
        jnp.transpose(w_pair, (0, 2, 1)),
        w_qkv,
        w_out,
    )


def body(peers, states, ancestors, noise, pair, token_mask, w_qkv, w_out, w_pair):
    part_count, tok_rows, width = states.shape
    one_each = part_count == peers and peers % 2 == 0 and tok_rows % 16 == 0 and peers * tok_rows == LANES and width % LANES == 0
    inner = functools.partial(particle_body, peers) if one_each else token_split_body
    return inner(states, ancestors, noise, pair, token_mask, w_qkv, w_out, w_pair)


def solution(mesh):
    placed = (
        P(("groups", "dom"), "tok", None),
        P(("groups", "dom")),
        P(("groups", "dom"), "tok", None),
        P(("groups", "tok"), None, None),
        P("groups"),
        P(),
        P(),
        P(),
    )
    return jax.shard_map(
        functools.partial(body, mesh.shape["tok"]),
        mesh=mesh,
        in_specs=placed,
        out_specs=P(("groups", "dom"), "tok", None),
        check_vma=False,
    )
```

```python
import functools

import jax
import jax.numpy as jnp
from jax import lax
from jax.experimental import pallas as pl
from jax.experimental.pallas import tpu as pltpu
from jax.sharding import PartitionSpec as P


def layer_norm(stream):
    values = stream.astype(jnp.float32)
    average = jnp.mean(values, axis=-1, keepdims=True)
    centred = values - average
    spread = jnp.mean(centred * centred, axis=-1, keepdims=True)
    return centred * lax.rsqrt(spread + 1e-05)


def token_split_body(states, ancestors, noise, pair, token_mask, w_qkv, w_out, w_pair):
    part_count = states.shape[0]
    tok_rows = states.shape[1]
    model_width = states.shape[2]
    head_count = w_pair.shape[2]
    head_width = model_width // head_count
    layer_count = w_qkv.shape[0]
    total_keys = pair.shape[1]
    everyone = lax.all_gather(states, "dom", axis=0, tiled=True)
    chosen = jnp.take(everyone, ancestors, axis=0)
    stream = (chosen.astype(jnp.float32) + 0.5 * noise.astype(jnp.float32)).astype(jnp.bfloat16)
    penalty = jnp.where(token_mask > 0, 0.0, -1000000000.0).astype(jnp.float32)
    pair_terms = jnp.einsum("ijc,lch->lhij", pair, w_pair, preferred_element_type=jnp.float32)
    full_bias = pair_terms + penalty[None, None, None, :]
    query_scale = head_width ** (-0.5)
    for layer_index in range(layer_count):
        normed = layer_norm(stream).astype(jnp.bfloat16)
        projected = jnp.dot(
            normed.reshape(part_count * tok_rows, model_width),
            w_qkv[layer_index],
            preferred_element_type=jnp.float32,
        )
        projected = projected.reshape(part_count, tok_rows, 3 * model_width)
        query = (projected[..., :model_width] * query_scale).astype(jnp.bfloat16)
        key_tiles = projected[..., model_width : 2 * model_width].astype(jnp.bfloat16)
        value_tiles = projected[..., 2 * model_width :].astype(jnp.bfloat16)
        layer_bias = full_bias[layer_index]
        query_heads = query.reshape(part_count, tok_rows, head_count, head_width)
        all_keys, all_values = (
            lax.all_gather(key_tiles, "tok", axis=1, tiled=True),
            lax.all_gather(value_tiles, "tok", axis=1, tiled=True),
        )
        key_heads = all_keys.reshape(part_count, total_keys, head_count, head_width)
        scores = (
            jnp.einsum(
                "pihe,pjhe->phij", query_heads, key_heads, preferred_element_type=jnp.float32
            )
            + layer_bias[None]
        )
        weights = jax.nn.softmax(scores, axis=-1).astype(jnp.bfloat16)
        value_heads = all_values.reshape(part_count, total_keys, head_count, head_width)
        attended = jnp.einsum(
            "phij,pjhe->pihe", weights, value_heads, preferred_element_type=jnp.float32
        ).astype(jnp.bfloat16)
        attended = attended.reshape(part_count * tok_rows, model_width)
        update = jnp.dot(attended, w_out[layer_index], preferred_element_type=jnp.float32)
        update = update.reshape(part_count, tok_rows, model_width)
        stream = (stream.astype(jnp.float32) + update).astype(jnp.bfloat16)
    return stream


MESH = pl.DeviceIdType.MESH
LANES = 128


def particle_kernel(
    peers,
    head_count,
    ancestors_hbm,
    states,
    noise_hbm,
    pair_hbm,
    mask_hbm,
    w_pair_hbm,
    w_qkv_hbm,
    w_out_hbm,
    result,
    ancestors,
    noise,
    pair,
    token_mask,
    w_pair,
    everyone,
    outgoing,
    stream_in,
    bias,
    bias_rows,
    qkv,
    score_rows,
    raised,
    finished,
    w_qkv,
    w_out,
    load_sem,
    weight_sem,
    state_sem,
    stream_send,
    stream_recv,
    bias_send,
    bias_recv,
    relay_send,
    relay_recv,
    out_send,
    out_recv,
):
    group = lax.axis_index("groups")
    me = lax.axis_index("tok")
    core = lax.axis_index("dom")
    sibling = (group, me, 1 - core)
    part_count, tok_rows, width = states.shape
    layer_count = w_qkv.shape[0]
    tokens = peers * tok_rows
    head_width = width // head_count
    half_heads = head_count // 2

    def ahead(step):
        return lax.rem(me + step, peers)

    def behind(step):
        return lax.rem(me + peers - step, peers)

    half = peers // 2
    side, place_in_half = me // half, lax.rem(me, half)
    far = [
        (half + step, (1 - side) * half + lax.rem(place_in_half + step, half))
        for step in range(half)
    ]
    near = [
        (step, side * half + lax.rem(place_in_half + step, half)) for step in range(1, half)
    ]
    exchanges = far + near

    def remote(source, target, send, recv, device):
        return pltpu.make_async_remote_copy(
            src_ref=source,
            dst_ref=target,
            send_sem=send,
            recv_sem=recv,
            device_id=device,
            device_id_type=MESH,
        )

    weight_copies = []
    for layer in range(layer_count):
        weight_copies.append(
            (
                pltpu.make_async_copy(w_qkv_hbm.at[layer], w_qkv.at[layer], weight_sem.at[layer, 0]),
                pltpu.make_async_copy(w_out_hbm.at[layer], w_out.at[layer], weight_sem.at[layer, 1]),
            )
        )
    mine = pl.ds(core * part_count, part_count)
    loads = []
    for place, (source, target) in enumerate(
        (
            (pair_hbm, pair),
            (w_pair_hbm, w_pair),
            (mask_hbm, token_mask),
            (ancestors_hbm, ancestors),
            (states, everyone.at[mine]),
            (noise_hbm, noise),
        )
    ):
        loads.append(pltpu.make_async_copy(source, target, load_sem.at[place]))
        loads[-1].start()

    barrier = pltpu.get_barrier_semaphore()
    pl.semaphore_signal(barrier, inc=1, device_id=sibling, device_id_type=MESH)
    for step in range(1, peers):
        pl.semaphore_signal(
            barrier, inc=1, device_id=(group, ahead(step), core), device_id_type=MESH
        )
    pl.semaphore_wait(barrier, peers)

    state_copy = remote(states, everyone.at[mine], state_sem.at[0], state_sem.at[1], sibling)
    state_copy.start()
    def make_bias(layer):
        penalty = jnp.where(token_mask[...] > 0, 0.0, -1000000000.0).astype(jnp.float32)
        pair_terms = lax.dot_general(
            w_pair[layer],
            pair[...].reshape(tok_rows * tokens, pair.shape[2]),
            (((1,), (1,)), ((), ())),
            preferred_element_type=jnp.float32,
        )
        for row in range(tok_rows):
            full = pair_terms[:, row * tokens : (row + 1) * tokens] + penalty
            bias_rows[:, row, :] = full - jnp.max(full, axis=-1, keepdims=True)
        bias[layer, me] = bias_rows[...].astype(jnp.bfloat16)

    my_heads = pl.ds(core * half_heads, half_heads)
    pairs = peers // 2
    partner = me + 1 - 2 * lax.rem(me, 2)
    bias_copies = []

    def send_bias(layer, slot, owner, target):
        block = bias.at[layer, owner, my_heads]
        copy = remote(
            block,
            block,
            bias_send.at[layer, slot],
            bias_recv.at[layer, slot],
            (group, target, core),
        )
        copy.start()
        bias_copies.append(copy)
        return copy

    def spread(layer):
        copies = [send_bias(layer, 0, me, partner)]
        for step in range(1, pairs):
            copies.append(send_bias(layer, step, me, ahead(2 * step)))
        return copies

    def hand_over(layer, slot, owner):
        block = bias.at[layer, owner, my_heads]
        copy = remote(
            block, block, relay_send.at[layer, slot], relay_recv.at[layer, slot], sibling
        )
        copy.start()
        return copy

    def relay_own_parity(layer, copies):
        handed = []
        for step in range(1, pairs):
            copies[step].wait_recv()
            copies.append(send_bias(layer, pairs - 1 + step, behind(2 * step), partner))
            handed.append(hand_over(layer, step, behind(2 * step)))
        copies[0].wait_recv()
        handed.append(hand_over(layer, 0, partner))
        return handed

    def relay_partner(layer, copies):
        handed = []
        for step in range(1, pairs):
            slot = pairs - 1 + step
            copies[slot].wait_recv()
            owner = lax.rem(partner + peers - 2 * step, peers)
            handed.append(hand_over(layer, slot, owner))
        return handed

    for load in loads[:3]:
        load.wait()
    make_bias(0)
    spreads = [spread(0)]
    relays = []
    for qkv_copy, out_copy in weight_copies:
        qkv_copy.start()
        out_copy.start()

    for load in loads[3:]:
        load.wait()
    state_copy.wait()

    def moved(particle):
        chosen = everyone[ancestors[particle]].astype(jnp.float32)
        return (chosen + 0.5 * noise[particle].astype(jnp.float32)).astype(jnp.bfloat16)

    stream_copies = []
    for step, target in exchanges:
        outgoing[step] = moved(target)
        copy = remote(
            outgoing.at[step],
            stream_in.at[me],
            stream_send.at[step],
            stream_recv.at[step],
            (group, target, core),
        )
        copy.start()
        stream_copies.append(copy)
    stream_in[me] = moved(me)

    for layer in range(1, layer_count):
        make_bias(layer)
    relays.append(relay_own_parity(0, spreads[0]))
    relays[0] += relay_partner(0, spreads[0])

    for copy in stream_copies:
        copy.wait_recv()

    def head_lanes(head, start, size):
        lanes = lax.broadcasted_iota(jnp.int32, (1, size), 1) + start
        inside = (lanes >= head * head_width) & (lanes < (head + 1) * head_width)
        return jnp.where(inside, 1.0, 0.0).astype(jnp.bfloat16)

    def attend(layer, first_block, blocks, kept_rows):
        rows = blocks * tok_rows
        tiles = []
        ready = 0
        for tile in range(width // LANES):
            start = tile * LANES
            first = start // head_width
            last = (start + LANES + head_width - 1) // head_width
            for head in range(ready, last):
                first_score = pl.multiple_of(head * tokens + first_block * tok_rows, tok_rows)
                bias_block = bias[layer, pl.ds(first_block, blocks), head]
                scores = score_rows[pl.ds(first_score, rows)] + bias_block.reshape(
                    rows, tokens
                ).astype(jnp.float32)
                largest = jnp.max(scores, axis=-1, keepdims=True)
                raised[kept_rows, pl.ds(head * tokens, tokens)] = jnp.exp(scores - largest).astype(
                    jnp.bfloat16
                )
            ready = last
            value = qkv[:, pl.ds(2 * width + start, LANES)]
            masks = [
                jnp.broadcast_to(head_lanes(head, start, LANES), (tokens, LANES))
                for head in range(first, last)
            ]
            sides = jnp.concatenate(
                [jnp.concatenate([value * mask, mask], axis=1) for mask in masks], axis=0
            )
            part = jnp.dot(
                raised[kept_rows, pl.ds(first * tokens, (last - first) * tokens)],
                sides,
                preferred_element_type=jnp.float32,
            )
            tiles.append((part[:, :LANES] / part[:, LANES:]).astype(jnp.bfloat16))
        return jnp.concatenate(tiles, axis=1)

    def project(layer, first_block, blocks, attended):
        update = jnp.dot(attended, w_out[layer], preferred_element_type=jnp.float32)
        old = stream_in[pl.ds(first_block, blocks)].astype(jnp.float32)
        return (old + update.reshape(old.shape)).astype(jnp.bfloat16)

    windows = []
    for head in range(head_count):
        if windows and (head + 1) * head_width <= windows[-1][0] + 2 * LANES:
            windows[-1][1].append(head)
        else:
            start = head * head_width // LANES * LANES
            windows.append((min(start, width - 2 * LANES), [head]))

    for layer in range(layer_count):
        if layer + 1 < layer_count:
            spreads.append(spread(layer + 1))
        stream = stream_in[...].reshape(tokens, width)
        normed = layer_norm(stream).astype(jnp.bfloat16)
        weight_copies[layer][0].wait()
        for block in range(3):
            columns = pl.ds(block * width, width)
            projected = jnp.dot(
                normed, w_qkv[layer, :, columns], preferred_element_type=jnp.float32
            )
            if block == 0:
                projected = projected * head_width ** (-0.5)
            qkv[:, columns] = projected.astype(jnp.bfloat16)
        for start, heads in windows:
            query = qkv[:, pl.ds(start, 2 * LANES)]
            score_rows[pl.ds(heads[0] * tokens, len(heads) * tokens)] = lax.dot_general(
                jnp.concatenate(
                    [query * head_lanes(head, start, 2 * LANES) for head in heads], axis=0
                ),
                qkv[:, pl.ds(width + start, 2 * LANES)],
                (((1,), (1,)), ((), ())),
                preferred_element_type=jnp.float32,
            )
        for copy in relays[layer]:
            copy.wait_recv()
        if layer + 1 < layer_count:
            relays.append(relay_own_parity(layer + 1, spreads[layer + 1]))
        if layer + 1 < layer_count:
            attended = attend(layer, 0, peers, pl.ds(0, tokens))
            relays[layer + 1] += relay_partner(layer + 1, spreads[layer + 1])
            weight_copies[layer][1].wait()
            stream_in[...] = project(layer, 0, peers, attended)

    last = layer_count - 1
    weight_copies[last][1].wait()
    out_copies = []
    for turn, (owner, exchange) in enumerate(((1 - side, far), (side, near))):
        first_block = owner * half
        kept_rows = pl.ds(turn * half * tok_rows, half * tok_rows)
        attended = attend(last, first_block, half, kept_rows)
        finished[pl.ds(first_block, half)] = project(last, first_block, half, attended)
        for slot, target in exchange:
            copy = remote(
                finished.at[target],
                result.at[me],
                out_send.at[slot],
                out_recv.at[slot],
                (group, target, core),
            )
            copy.start()
            out_copies.append(copy)
    kept = pltpu.make_async_copy(finished.at[me], result.at[me], load_sem.at[6])
    kept.start()
    kept.wait()
    for copies in [stream_copies, bias_copies] + relays:
        for copy in copies:
            copy.wait_send()
    for copy in out_copies:
        copy.wait()


def particle_body(peers, states, ancestors, noise, pair, token_mask, w_qkv, w_out, w_pair):
    part_count, tok_rows, width = states.shape
    layer_count, _, head_count = w_pair.shape
    tokens = peers * tok_rows
    hbm = pl.BlockSpec(memory_space=pltpu.HBM)
    dma = pltpu.SemaphoreType.DMA
    per_peer, per_layer = dma((peers,)), dma((layer_count, peers))
    return pl.pallas_call(
        functools.partial(particle_kernel, peers, head_count),
        out_shape=jax.ShapeDtypeStruct(states.shape, states.dtype),
        in_specs=[hbm] * 8,
        out_specs=hbm,
        scratch_shapes=[
            pltpu.SMEM(ancestors.shape, ancestors.dtype),
            pltpu.VMEM(noise.shape, noise.dtype),
            pltpu.VMEM(pair.shape, pair.dtype),
            pltpu.VMEM((1, tokens), token_mask.dtype),
            pltpu.VMEM((layer_count, head_count, w_pair.shape[1]), w_pair.dtype),
            pltpu.VMEM((2 * part_count, tok_rows, width), jnp.bfloat16),
            pltpu.VMEM((peers, tok_rows, width), jnp.bfloat16),
            pltpu.VMEM((peers, tok_rows, width), jnp.bfloat16),
            pltpu.VMEM((layer_count, peers, head_count, tok_rows, tokens), jnp.bfloat16),
            pltpu.VMEM((head_count, tok_rows, tokens), jnp.float32),
            pltpu.VMEM((tokens, 3 * width), jnp.bfloat16),
            pltpu.VMEM((head_count * tokens, tokens), jnp.float32),
            pltpu.VMEM((tokens, head_count * tokens), jnp.bfloat16),
            pltpu.VMEM((peers, tok_rows, width), jnp.bfloat16),
            pltpu.VMEM(w_qkv.shape, w_qkv.dtype),
            pltpu.VMEM(w_out.shape, w_out.dtype),
            dma((7,)),
            dma((layer_count, 2)),
            dma((2,)),
            per_peer,
            per_peer,
            per_layer,
            per_layer,
            per_layer,
            per_layer,
            per_peer,
            per_peer,
        ],
        compiler_params=pltpu.CompilerParams(
            collective_id=0, has_side_effects=True, vmem_limit_bytes=63 * 1024 * 1024
        ),
        name="particle_layers",
    )(
        ancestors,
        states,
        noise,
        pair,
        token_mask.reshape(1, tokens),
        jnp.transpose(w_pair, (0, 2, 1)),
        w_qkv,
        w_out,
    )


def body(peers, states, ancestors, noise, pair, token_mask, w_qkv, w_out, w_pair):
    part_count, tok_rows, width = states.shape
    one_each = part_count == peers and peers % 2 == 0 and tok_rows % 16 == 0 and peers * tok_rows == LANES and width % LANES == 0
    inner = functools.partial(particle_body, peers) if one_each else token_split_body
    return inner(states, ancestors, noise, pair, token_mask, w_qkv, w_out, w_pair)


def solution(mesh):
    placed = (
        P(("groups", "dom"), "tok", None),
        P(("groups", "dom")),
        P(("groups", "dom"), "tok", None),
        P(("groups", "tok"), None, None),
        P("groups"),
        P(),
        P(),
        P(),
    )
    return jax.shard_map(
        functools.partial(body, mesh.shape["tok"]),
        mesh=mesh,
        in_specs=placed,
        out_specs=P(("groups", "dom"), "tok", None),
        check_vma=False,
    )
```

```python
import functools

import jax
import jax.numpy as jnp
from jax import lax
from jax.experimental import pallas as pl
from jax.experimental.pallas import tpu as pltpu
from jax.sharding import PartitionSpec as P


def layer_norm(stream):
    values = stream.astype(jnp.float32)
    average = jnp.mean(values, axis=-1, keepdims=True)
    centred = values - average
    spread = jnp.mean(centred * centred, axis=-1, keepdims=True)
    return centred * lax.rsqrt(spread + 1e-05)


def token_split_body(states, ancestors, noise, pair, token_mask, w_qkv, w_out, w_pair):
    part_count = states.shape[0]
    tok_rows = states.shape[1]
    model_width = states.shape[2]
    head_count = w_pair.shape[2]
    head_width = model_width // head_count
    layer_count = w_qkv.shape[0]
    total_keys = pair.shape[1]
    everyone = lax.all_gather(states, "dom", axis=0, tiled=True)
    chosen = jnp.take(everyone, ancestors, axis=0)
    stream = (chosen.astype(jnp.float32) + 0.5 * noise.astype(jnp.float32)).astype(jnp.bfloat16)
    penalty = jnp.where(token_mask > 0, 0.0, -1000000000.0).astype(jnp.float32)
    pair_terms = jnp.einsum("ijc,lch->lhij", pair, w_pair, preferred_element_type=jnp.float32)
    full_bias = pair_terms + penalty[None, None, None, :]
    query_scale = head_width ** (-0.5)
    for layer_index in range(layer_count):
        normed = layer_norm(stream).astype(jnp.bfloat16)
        projected = jnp.dot(
            normed.reshape(part_count * tok_rows, model_width),
            w_qkv[layer_index],
            preferred_element_type=jnp.float32,
        )
        projected = projected.reshape(part_count, tok_rows, 3 * model_width)
        query = (projected[..., :model_width] * query_scale).astype(jnp.bfloat16)
        key_tiles = projected[..., model_width : 2 * model_width].astype(jnp.bfloat16)
        value_tiles = projected[..., 2 * model_width :].astype(jnp.bfloat16)
        layer_bias = full_bias[layer_index]
        query_heads = query.reshape(part_count, tok_rows, head_count, head_width)
        all_keys, all_values = (
            lax.all_gather(key_tiles, "tok", axis=1, tiled=True),
            lax.all_gather(value_tiles, "tok", axis=1, tiled=True),
        )
        key_heads = all_keys.reshape(part_count, total_keys, head_count, head_width)
        scores = (
            jnp.einsum(
                "pihe,pjhe->phij", query_heads, key_heads, preferred_element_type=jnp.float32
            )
            + layer_bias[None]
        )
        weights = jax.nn.softmax(scores, axis=-1).astype(jnp.bfloat16)
        value_heads = all_values.reshape(part_count, total_keys, head_count, head_width)
        attended = jnp.einsum(
            "phij,pjhe->pihe", weights, value_heads, preferred_element_type=jnp.float32
        ).astype(jnp.bfloat16)
        attended = attended.reshape(part_count * tok_rows, model_width)
        update = jnp.dot(attended, w_out[layer_index], preferred_element_type=jnp.float32)
        update = update.reshape(part_count, tok_rows, model_width)
        stream = (stream.astype(jnp.float32) + update).astype(jnp.bfloat16)
    return stream


MESH = pl.DeviceIdType.MESH
LANES = 128


def particle_kernel(
    peers,
    head_count,
    ancestors_hbm,
    states,
    noise_hbm,
    pair_hbm,
    mask_hbm,
    w_pair_hbm,
    w_qkv_hbm,
    w_out_hbm,
    result,
    ancestors,
    noise,
    pair,
    token_mask,
    w_pair,
    everyone,
    outgoing,
    stream_in,
    bias,
    bias_rows,
    qkv,
    score_rows,
    raised,
    finished,
    w_qkv,
    w_out,
    load_sem,
    weight_sem,
    state_sem,
    stream_send,
    stream_recv,
    bias_send,
    bias_recv,
    relay_send,
    relay_recv,
    out_send,
    out_recv,
):
    group = lax.axis_index("groups")
    me = lax.axis_index("tok")
    core = lax.axis_index("dom")
    sibling = (group, me, 1 - core)
    part_count, tok_rows, width = states.shape
    layer_count = w_qkv.shape[0]
    tokens = peers * tok_rows
    head_width = width // head_count
    half_heads = head_count // 2

    def ahead(step):
        return lax.rem(me + step, peers)

    def behind(step):
        return lax.rem(me + peers - step, peers)

    half = peers // 2
    side, place_in_half = me // half, lax.rem(me, half)
    far = [
        (half + step, (1 - side) * half + lax.rem(place_in_half + step, half))
        for step in range(half)
    ]
    near = [
        (step, side * half + lax.rem(place_in_half + step, half)) for step in range(1, half)
    ]
    exchanges = near + far

    def remote(source, target, send, recv, device):
        return pltpu.make_async_remote_copy(
            src_ref=source,
            dst_ref=target,
            send_sem=send,
            recv_sem=recv,
            device_id=device,
            device_id_type=MESH,
        )

    weight_copies = []
    for layer in range(layer_count):
        weight_copies.append(
            (
                pltpu.make_async_copy(w_qkv_hbm.at[layer], w_qkv.at[layer], weight_sem.at[layer, 0]),
                pltpu.make_async_copy(w_out_hbm.at[layer], w_out.at[layer], weight_sem.at[layer, 1]),
            )
        )
    mine = pl.ds(core * part_count, part_count)
    loads = []
    for place, (source, target) in enumerate(
        (
            (pair_hbm, pair),
            (w_pair_hbm, w_pair),
            (mask_hbm, token_mask),
            (ancestors_hbm, ancestors),
            (states, everyone.at[mine]),
            (noise_hbm, noise),
        )
    ):
        loads.append(pltpu.make_async_copy(source, target, load_sem.at[place]))
        loads[-1].start()

    barrier = pltpu.get_barrier_semaphore()
    pl.semaphore_signal(barrier, inc=1, device_id=sibling, device_id_type=MESH)
    for step in range(1, peers):
        pl.semaphore_signal(
            barrier, inc=1, device_id=(group, ahead(step), core), device_id_type=MESH
        )
    pl.semaphore_wait(barrier, peers)

    state_copy = remote(states, everyone.at[mine], state_sem.at[0], state_sem.at[1], sibling)
    state_copy.start()
    def make_bias(layer):
        penalty = jnp.where(token_mask[...] > 0, 0.0, -1000000000.0).astype(jnp.float32)
        pair_terms = lax.dot_general(
            w_pair[layer],
            pair[...].reshape(tok_rows * tokens, pair.shape[2]),
            (((1,), (1,)), ((), ())),
            preferred_element_type=jnp.float32,
        )
        for row in range(tok_rows):
            full = pair_terms[:, row * tokens : (row + 1) * tokens] + penalty
            bias_rows[:, row, :] = full - jnp.max(full, axis=-1, keepdims=True)
        bias[layer, me] = bias_rows[...].astype(jnp.bfloat16)

    my_heads = pl.ds(core * half_heads, half_heads)
    pairs = peers // 2
    partner = me + 1 - 2 * lax.rem(me, 2)
    bias_copies = []

    def send_bias(layer, slot, owner, target):
        block = bias.at[layer, owner, my_heads]
        copy = remote(
            block,
            block,
            bias_send.at[layer, slot],
            bias_recv.at[layer, slot],
            (group, target, core),
        )
        copy.start()
        bias_copies.append(copy)
        return copy

    def spread(layer):
        copies = [send_bias(layer, 0, me, partner)]
        for step in range(1, pairs):
            copies.append(send_bias(layer, step, me, ahead(2 * step)))
        return copies

    def hand_over(layer, slot, owner):
        block = bias.at[layer, owner, my_heads]
        copy = remote(
            block, block, relay_send.at[layer, slot], relay_recv.at[layer, slot], sibling
        )
        copy.start()
        return copy

    def relay_own_parity(layer, copies):
        handed = []
        for step in range(1, pairs):
            copies[step].wait_recv()
            copies.append(send_bias(layer, pairs - 1 + step, behind(2 * step), partner))
            handed.append(hand_over(layer, step, behind(2 * step)))
        copies[0].wait_recv()
        handed.append(hand_over(layer, 0, partner))
        return handed

    def relay_partner(layer, copies):
        handed = []
        for step in range(1, pairs):
            slot = pairs - 1 + step
            copies[slot].wait_recv()
            owner = lax.rem(partner + peers - 2 * step, peers)
            handed.append(hand_over(layer, slot, owner))
        return handed

    for load in loads[:3]:
        load.wait()
    make_bias(0)
    spreads = [spread(0)]
    relays = []
    for qkv_copy, out_copy in weight_copies:
        qkv_copy.start()
        out_copy.start()

    for load in loads[3:]:
        load.wait()
    state_copy.wait()

    def moved(particle):
        chosen = everyone[ancestors[particle]].astype(jnp.float32)
        return (chosen + 0.5 * noise[particle].astype(jnp.float32)).astype(jnp.bfloat16)

    stream_copies = []
    for step, target in exchanges:
        outgoing[step] = moved(target)
        copy = remote(
            outgoing.at[step],
            stream_in.at[me],
            stream_send.at[step],
            stream_recv.at[step],
            (group, target, core),
        )
        copy.start()
        stream_copies.append(copy)
    stream_in[me] = moved(me)

    for layer in range(1, layer_count):
        make_bias(layer)
    relays.append(relay_own_parity(0, spreads[0]))
    def head_lanes(head, start, size):
        lanes = lax.broadcasted_iota(jnp.int32, (1, size), 1) + start
        inside = (lanes >= head * head_width) & (lanes < (head + 1) * head_width)
        return jnp.where(inside, 1.0, 0.0).astype(jnp.bfloat16)

    def attend(layer, first_block, blocks, kept_rows):
        rows = blocks * tok_rows
        tiles = []
        ready = 0
        for tile in range(width // LANES):
            start = tile * LANES
            first = start // head_width
            last = (start + LANES + head_width - 1) // head_width
            for head in range(ready, last):
                first_score = pl.multiple_of(head * tokens + first_block * tok_rows, tok_rows)
                bias_block = bias[layer, pl.ds(first_block, blocks), head]
                scores = score_rows[pl.ds(first_score, rows)] + bias_block.reshape(
                    rows, tokens
                ).astype(jnp.float32)
                largest = jnp.max(scores, axis=-1, keepdims=True)
                raised[kept_rows, pl.ds(head * tokens, tokens)] = jnp.exp(scores - largest).astype(
                    jnp.bfloat16
                )
            ready = last
            value = qkv[:, pl.ds(2 * width + start, LANES)]
            masks = [
                jnp.broadcast_to(head_lanes(head, start, LANES), (tokens, LANES))
                for head in range(first, last)
            ]
            sides = jnp.concatenate(
                [jnp.concatenate([value * mask, mask], axis=1) for mask in masks], axis=0
            )
            part = jnp.dot(
                raised[kept_rows, pl.ds(first * tokens, (last - first) * tokens)],
                sides,
                preferred_element_type=jnp.float32,
            )
            tiles.append((part[:, :LANES] / part[:, LANES:]).astype(jnp.bfloat16))
        return jnp.concatenate(tiles, axis=1)

    def project(layer, first_block, blocks, attended):
        update = jnp.dot(attended, w_out[layer], preferred_element_type=jnp.float32)
        old = stream_in[pl.ds(first_block, blocks)].astype(jnp.float32)
        return (old + update.reshape(old.shape)).astype(jnp.bfloat16)

    def make_qkv(layer, first_block, blocks):
        rows = blocks * tok_rows
        first_row = first_block * tok_rows
        if blocks < peers:
            first_row = pl.multiple_of(first_row, rows)
        stream = stream_in[pl.ds(first_block, blocks)].reshape(rows, width)
        normed = layer_norm(stream).astype(jnp.bfloat16)
        for block in range(3):
            columns = pl.ds(block * width, width)
            projected = jnp.dot(
                normed, w_qkv[layer, :, columns], preferred_element_type=jnp.float32
            )
            if block == 0:
                projected = projected * head_width ** (-0.5)
            qkv[pl.ds(first_row, rows), columns] = projected.astype(jnp.bfloat16)

    windows = []
    for head in range(head_count):
        if windows and (head + 1) * head_width <= windows[-1][0] + 2 * LANES:
            windows[-1][1].append(head)
        else:
            start = head * head_width // LANES * LANES
            windows.append((min(start, width - 2 * LANES), [head]))

    for layer in range(layer_count):
        if layer == 0:
            for copy in stream_copies[: half - 1]:
                copy.wait_recv()
            weight_copies[0][0].wait()
            make_qkv(0, side * half, half)
            relays[0] += relay_partner(0, spreads[0])
            for copy in stream_copies[half - 1 :]:
                copy.wait_recv()
            if layer + 1 < layer_count:
                spreads.append(spread(layer + 1))
            make_qkv(0, (1 - side) * half, half)
        else:
            if layer + 1 < layer_count:
                spreads.append(spread(layer + 1))
            weight_copies[layer][0].wait()
            make_qkv(layer, 0, peers)
        for start, heads in windows:
            query = qkv[:, pl.ds(start, 2 * LANES)]
            score_rows[pl.ds(heads[0] * tokens, len(heads) * tokens)] = lax.dot_general(
                jnp.concatenate(
                    [query * head_lanes(head, start, 2 * LANES) for head in heads], axis=0
                ),
                qkv[:, pl.ds(width + start, 2 * LANES)],
                (((1,), (1,)), ((), ())),
                preferred_element_type=jnp.float32,
            )
        for copy in relays[layer]:
            copy.wait_recv()
        if layer + 1 < layer_count:
            relays.append(relay_own_parity(layer + 1, spreads[layer + 1]))
        if layer + 1 < layer_count:
            attended = attend(layer, 0, peers, pl.ds(0, tokens))
            relays[layer + 1] += relay_partner(layer + 1, spreads[layer + 1])
            weight_copies[layer][1].wait()
            stream_in[...] = project(layer, 0, peers, attended)

    last = layer_count - 1
    weight_copies[last][1].wait()
    out_copies = []
    for turn, (owner, exchange) in enumerate(((1 - side, far), (side, near))):
        first_block = owner * half
        kept_rows = pl.ds(turn * half * tok_rows, half * tok_rows)
        attended = attend(last, first_block, half, kept_rows)
        finished[pl.ds(first_block, half)] = project(last, first_block, half, attended)
        for slot, target in exchange:
            copy = remote(
                finished.at[target],
                result.at[me],
                out_send.at[slot],
                out_recv.at[slot],
                (group, target, core),
            )
            copy.start()
            out_copies.append(copy)
    kept = pltpu.make_async_copy(finished.at[me], result.at[me], load_sem.at[6])
    kept.start()
    kept.wait()
    for copies in [stream_copies, bias_copies] + relays:
        for copy in copies:
            copy.wait_send()
    for copy in out_copies:
        copy.wait()


def particle_body(peers, states, ancestors, noise, pair, token_mask, w_qkv, w_out, w_pair):
    part_count, tok_rows, width = states.shape
    layer_count, _, head_count = w_pair.shape
    tokens = peers * tok_rows
    hbm = pl.BlockSpec(memory_space=pltpu.HBM)
    dma = pltpu.SemaphoreType.DMA
    per_peer, per_layer = dma((peers,)), dma((layer_count, peers))
    return pl.pallas_call(
        functools.partial(particle_kernel, peers, head_count),
        out_shape=jax.ShapeDtypeStruct(states.shape, states.dtype),
        in_specs=[hbm] * 8,
        out_specs=hbm,
        scratch_shapes=[
            pltpu.SMEM(ancestors.shape, ancestors.dtype),
            pltpu.VMEM(noise.shape, noise.dtype),
            pltpu.VMEM(pair.shape, pair.dtype),
            pltpu.VMEM((1, tokens), token_mask.dtype),
            pltpu.VMEM((layer_count, head_count, w_pair.shape[1]), w_pair.dtype),
            pltpu.VMEM((2 * part_count, tok_rows, width), jnp.bfloat16),
            pltpu.VMEM((peers, tok_rows, width), jnp.bfloat16),
            pltpu.VMEM((peers, tok_rows, width), jnp.bfloat16),
            pltpu.VMEM((layer_count, peers, head_count, tok_rows, tokens), jnp.bfloat16),
            pltpu.VMEM((head_count, tok_rows, tokens), jnp.float32),
            pltpu.VMEM((tokens, 3 * width), jnp.bfloat16),
            pltpu.VMEM((head_count * tokens, tokens), jnp.float32),
            pltpu.VMEM((tokens, head_count * tokens), jnp.bfloat16),
            pltpu.VMEM((peers, tok_rows, width), jnp.bfloat16),
            pltpu.VMEM(w_qkv.shape, w_qkv.dtype),
            pltpu.VMEM(w_out.shape, w_out.dtype),
            dma((7,)),
            dma((layer_count, 2)),
            dma((2,)),
            per_peer,
            per_peer,
            per_layer,
            per_layer,
            per_layer,
            per_layer,
            per_peer,
            per_peer,
        ],
        compiler_params=pltpu.CompilerParams(
            collective_id=0, has_side_effects=True, vmem_limit_bytes=63 * 1024 * 1024
        ),
        name="particle_layers",
    )(
        ancestors,
        states,
        noise,
        pair,
        token_mask.reshape(1, tokens),
        jnp.transpose(w_pair, (0, 2, 1)),
        w_qkv,
        w_out,
    )


def body(peers, states, ancestors, noise, pair, token_mask, w_qkv, w_out, w_pair):
    part_count, tok_rows, width = states.shape
    one_each = part_count == peers and peers % 2 == 0 and tok_rows % 16 == 0 and peers * tok_rows == LANES and width % LANES == 0
    inner = functools.partial(particle_body, peers) if one_each else token_split_body
    return inner(states, ancestors, noise, pair, token_mask, w_qkv, w_out, w_pair)


def solution(mesh):
    placed = (
        P(("groups", "dom"), "tok", None),
        P(("groups", "dom")),
        P(("groups", "dom"), "tok", None),
        P(("groups", "tok"), None, None),
        P("groups"),
        P(),
        P(),
        P(),
    )
    return jax.shard_map(
        functools.partial(body, mesh.shape["tok"]),
        mesh=mesh,
        in_specs=placed,
        out_specs=P(("groups", "dom"), "tok", None),
        check_vma=False,
    )
```

```python
import functools

import jax
import jax.numpy as jnp
from jax import lax
from jax.experimental import pallas as pl
from jax.experimental.pallas import tpu as pltpu
from jax.sharding import PartitionSpec as P


def layer_norm(stream):
    values = stream.astype(jnp.float32)
    average = jnp.mean(values, axis=-1, keepdims=True)
    centred = values - average
    spread = jnp.mean(centred * centred, axis=-1, keepdims=True)
    return centred * lax.rsqrt(spread + 1e-05)


def token_split_body(states, ancestors, noise, pair, token_mask, w_qkv, w_out, w_pair):
    part_count = states.shape[0]
    tok_rows = states.shape[1]
    model_width = states.shape[2]
    head_count = w_pair.shape[2]
    head_width = model_width // head_count
    layer_count = w_qkv.shape[0]
    total_keys = pair.shape[1]
    everyone = lax.all_gather(states, "dom", axis=0, tiled=True)
    chosen = jnp.take(everyone, ancestors, axis=0)
    stream = (chosen.astype(jnp.float32) + 0.5 * noise.astype(jnp.float32)).astype(jnp.bfloat16)
    penalty = jnp.where(token_mask > 0, 0.0, -1000000000.0).astype(jnp.float32)
    pair_terms = jnp.einsum("ijc,lch->lhij", pair, w_pair, preferred_element_type=jnp.float32)
    full_bias = pair_terms + penalty[None, None, None, :]
    query_scale = head_width ** (-0.5)
    for layer_index in range(layer_count):
        normed = layer_norm(stream).astype(jnp.bfloat16)
        projected = jnp.dot(
            normed.reshape(part_count * tok_rows, model_width),
            w_qkv[layer_index],
            preferred_element_type=jnp.float32,
        )
        projected = projected.reshape(part_count, tok_rows, 3 * model_width)
        query = (projected[..., :model_width] * query_scale).astype(jnp.bfloat16)
        key_tiles = projected[..., model_width : 2 * model_width].astype(jnp.bfloat16)
        value_tiles = projected[..., 2 * model_width :].astype(jnp.bfloat16)
        layer_bias = full_bias[layer_index]
        query_heads = query.reshape(part_count, tok_rows, head_count, head_width)
        all_keys, all_values = (
            lax.all_gather(key_tiles, "tok", axis=1, tiled=True),
            lax.all_gather(value_tiles, "tok", axis=1, tiled=True),
        )
        key_heads = all_keys.reshape(part_count, total_keys, head_count, head_width)
        scores = (
            jnp.einsum(
                "pihe,pjhe->phij", query_heads, key_heads, preferred_element_type=jnp.float32
            )
            + layer_bias[None]
        )
        weights = jax.nn.softmax(scores, axis=-1).astype(jnp.bfloat16)
        value_heads = all_values.reshape(part_count, total_keys, head_count, head_width)
        attended = jnp.einsum(
            "phij,pjhe->pihe", weights, value_heads, preferred_element_type=jnp.float32
        ).astype(jnp.bfloat16)
        attended = attended.reshape(part_count * tok_rows, model_width)
        update = jnp.dot(attended, w_out[layer_index], preferred_element_type=jnp.float32)
        update = update.reshape(part_count, tok_rows, model_width)
        stream = (stream.astype(jnp.float32) + update).astype(jnp.bfloat16)
    return stream


MESH = pl.DeviceIdType.MESH
LANES = 128


def particle_kernel(
    peers,
    head_count,
    ancestors_hbm,
    states,
    noise_hbm,
    pair_hbm,
    mask_hbm,
    w_pair_hbm,
    w_qkv_hbm,
    w_out_hbm,
    result,
    ancestors,
    noise,
    pair,
    token_mask,
    w_pair,
    everyone,
    outgoing,
    stream_in,
    bias,
    bias_rows,
    qkv,
    score_rows,
    raised,
    finished,
    w_qkv,
    w_out,
    load_sem,
    weight_sem,
    state_sem,
    stream_send,
    stream_recv,
    bias_send,
    bias_recv,
    relay_send,
    relay_recv,
    out_send,
    out_recv,
):
    group = lax.axis_index("groups")
    me = lax.axis_index("tok")
    core = lax.axis_index("dom")
    sibling = (group, me, 1 - core)
    part_count, tok_rows, width = states.shape
    layer_count = w_qkv.shape[0]
    tokens = peers * tok_rows
    head_width = width // head_count
    half_heads = head_count // 2

    def ahead(step):
        return lax.rem(me + step, peers)

    def behind(step):
        return lax.rem(me + peers - step, peers)

    half = peers // 2
    side, place_in_half = me // half, lax.rem(me, half)
    far = [
        (half + step, (1 - side) * half + lax.rem(place_in_half + step, half))
        for step in range(half)
    ]
    near = [
        (step, side * half + lax.rem(place_in_half + step, half)) for step in range(1, half)
    ]
    exchanges = near + far

    def remote(source, target, send, recv, device):
        return pltpu.make_async_remote_copy(
            src_ref=source,
            dst_ref=target,
            send_sem=send,
            recv_sem=recv,
            device_id=device,
            device_id_type=MESH,
        )

    weight_copies = []
    for layer in range(layer_count):
        weight_copies.append(
            (
                pltpu.make_async_copy(w_qkv_hbm.at[layer], w_qkv.at[layer], weight_sem.at[layer, 0]),
                pltpu.make_async_copy(w_out_hbm.at[layer], w_out.at[layer], weight_sem.at[layer, 1]),
            )
        )
    mine = pl.ds(core * part_count, part_count)
    loads = []
    for place, (source, target) in enumerate(
        (
            (pair_hbm, pair),
            (w_pair_hbm, w_pair),
            (mask_hbm, token_mask),
            (ancestors_hbm, ancestors),
            (states, everyone.at[mine]),
            (noise_hbm, noise),
        )
    ):
        loads.append(pltpu.make_async_copy(source, target, load_sem.at[place]))
        loads[-1].start()
    weight_copies[0][0].start()

    barrier = pltpu.get_barrier_semaphore()
    pl.semaphore_signal(barrier, inc=1, device_id=sibling, device_id_type=MESH)
    for step in range(1, peers):
        pl.semaphore_signal(
            barrier, inc=1, device_id=(group, ahead(step), core), device_id_type=MESH
        )
    pl.semaphore_wait(barrier, peers)

    state_copies = []
    share = part_count // 2
    for piece in range(2):
        copy = remote(
            states.at[pl.ds(piece * share, share)],
            everyone.at[pl.ds(core * part_count + piece * share, share)],
            state_sem.at[0, piece],
            state_sem.at[1, piece],
            sibling,
        )
        copy.start()
        state_copies.append(copy)
    def make_bias(layer):
        penalty = jnp.where(token_mask[...] > 0, 0.0, -1000000000.0).astype(jnp.float32)
        pair_terms = lax.dot_general(
            w_pair[layer],
            pair[...].reshape(tok_rows * tokens, pair.shape[2]),
            (((1,), (1,)), ((), ())),
            preferred_element_type=jnp.float32,
        )
        for row in range(tok_rows):
            full = pair_terms[:, row * tokens : (row + 1) * tokens] + penalty
            bias_rows[:, row, :] = full - jnp.max(full, axis=-1, keepdims=True)
        bias[layer, me] = bias_rows[...].astype(jnp.bfloat16)

    my_heads = pl.ds(core * half_heads, half_heads)
    pairs = peers // 2
    partner = me + 1 - 2 * lax.rem(me, 2)
    bias_copies = []

    def send_bias(layer, slot, owner, target):
        block = bias.at[layer, owner, my_heads]
        copy = remote(
            block,
            block,
            bias_send.at[layer, slot],
            bias_recv.at[layer, slot],
            (group, target, core),
        )
        copy.start()
        bias_copies.append(copy)
        return copy

    def spread(layer):
        copies = [send_bias(layer, 0, me, partner)]
        for step in range(1, pairs):
            copies.append(send_bias(layer, step, me, ahead(2 * step)))
        return copies

    def hand_over(layer, slot, owner):
        block = bias.at[layer, owner, my_heads]
        copy = remote(
            block, block, relay_send.at[layer, slot], relay_recv.at[layer, slot], sibling
        )
        copy.start()
        return copy

    def relay_own_parity(layer, copies):
        handed = []
        for step in range(1, pairs):
            copies[step].wait_recv()
            copies.append(send_bias(layer, pairs - 1 + step, behind(2 * step), partner))
            handed.append(hand_over(layer, step, behind(2 * step)))
        copies[0].wait_recv()
        handed.append(hand_over(layer, 0, partner))
        return handed

    def relay_partner(layer, copies):
        handed = []
        for step in range(1, pairs):
            slot = pairs - 1 + step
            copies[slot].wait_recv()
            owner = lax.rem(partner + peers - 2 * step, peers)
            handed.append(hand_over(layer, slot, owner))
        return handed

    for load in loads[:3]:
        load.wait()
    make_bias(0)
    spreads = [spread(0)]
    relays = []

    for load in loads[3:]:
        load.wait()
    for copy in state_copies:
        copy.wait()

    def moved(particle):
        chosen = everyone[ancestors[particle]].astype(jnp.float32)
        return (chosen + 0.5 * noise[particle].astype(jnp.float32)).astype(jnp.bfloat16)

    stream_copies = []
    for step, target in exchanges:
        outgoing[step] = moved(target)
        copy = remote(
            outgoing.at[step],
            stream_in.at[me],
            stream_send.at[step],
            stream_recv.at[step],
            (group, target, core),
        )
        copy.start()
        stream_copies.append(copy)
    stream_in[me] = moved(me)
    for layer in range(layer_count):
        if layer > 0:
            weight_copies[layer][0].start()
        weight_copies[layer][1].start()

    for layer in range(1, layer_count):
        make_bias(layer)
    relays.append(relay_own_parity(0, spreads[0]))
    def head_lanes(head, start, size):
        lanes = lax.broadcasted_iota(jnp.int32, (1, size), 1) + start
        inside = (lanes >= head * head_width) & (lanes < (head + 1) * head_width)
        return jnp.where(inside, 1.0, 0.0).astype(jnp.bfloat16)

    def attend(layer, first_block, blocks, kept_rows):
        rows = blocks * tok_rows
        tiles = []
        ready = 0
        for tile in range(width // LANES):
            start = tile * LANES
            first = start // head_width
            last = (start + LANES + head_width - 1) // head_width
            for head in range(ready, last):
                first_score = pl.multiple_of(head * tokens + first_block * tok_rows, tok_rows)
                bias_block = bias[layer, pl.ds(first_block, blocks), head]
                scores = score_rows[pl.ds(first_score, rows)] + bias_block.reshape(
                    rows, tokens
                ).astype(jnp.float32)
                largest = jnp.max(scores, axis=-1, keepdims=True)
                raised[kept_rows, pl.ds(head * tokens, tokens)] = jnp.exp(scores - largest).astype(
                    jnp.bfloat16
                )
            ready = last
            value = qkv[:, pl.ds(2 * width + start, LANES)]
            masks = [
                jnp.broadcast_to(head_lanes(head, start, LANES), (tokens, LANES))
                for head in range(first, last)
            ]
            sides = jnp.concatenate(
                [jnp.concatenate([value * mask, mask], axis=1) for mask in masks], axis=0
            )
            part = jnp.dot(
                raised[kept_rows, pl.ds(first * tokens, (last - first) * tokens)],
                sides,
                preferred_element_type=jnp.float32,
            )
            tiles.append((part[:, :LANES] / part[:, LANES:]).astype(jnp.bfloat16))
        return jnp.concatenate(tiles, axis=1)

    def project(layer, first_block, blocks, attended):
        update = jnp.dot(attended, w_out[layer], preferred_element_type=jnp.float32)
        old = stream_in[pl.ds(first_block, blocks)].astype(jnp.float32)
        return (old + update.reshape(old.shape)).astype(jnp.bfloat16)

    def make_qkv(layer, first_block, blocks):
        rows = blocks * tok_rows
        first_row = first_block * tok_rows
        if blocks < peers:
            first_row = pl.multiple_of(first_row, rows)
        stream = stream_in[pl.ds(first_block, blocks)].reshape(rows, width)
        normed = layer_norm(stream).astype(jnp.bfloat16)
        for block in range(3):
            columns = pl.ds(block * width, width)
            projected = jnp.dot(
                normed, w_qkv[layer, :, columns], preferred_element_type=jnp.float32
            )
            if block == 0:
                projected = projected * head_width ** (-0.5)
            qkv[pl.ds(first_row, rows), columns] = projected.astype(jnp.bfloat16)

    windows = []
    for head in range(head_count):
        if windows and (head + 1) * head_width <= windows[-1][0] + 2 * LANES:
            windows[-1][1].append(head)
        else:
            start = head * head_width // LANES * LANES
            windows.append((min(start, width - 2 * LANES), [head]))

    for layer in range(layer_count):
        if layer == 0:
            for copy in stream_copies[: half - 1]:
                copy.wait_recv()
            weight_copies[0][0].wait()
            make_qkv(0, side * half, half)
            relays[0] += relay_partner(0, spreads[0])
            for copy in stream_copies[half - 1 :]:
                copy.wait_recv()
            if layer + 1 < layer_count:
                spreads.append(spread(layer + 1))
            make_qkv(0, (1 - side) * half, half)
        else:
            if layer + 1 < layer_count:
                spreads.append(spread(layer + 1))
            weight_copies[layer][0].wait()
            make_qkv(layer, 0, peers)
        for start, heads in windows:
            query = qkv[:, pl.ds(start, 2 * LANES)]
            score_rows[pl.ds(heads[0] * tokens, len(heads) * tokens)] = lax.dot_general(
                jnp.concatenate(
                    [query * head_lanes(head, start, 2 * LANES) for head in heads], axis=0
                ),
                qkv[:, pl.ds(width + start, 2 * LANES)],
                (((1,), (1,)), ((), ())),
                preferred_element_type=jnp.float32,
            )
        for copy in relays[layer]:
            copy.wait_recv()
        if layer + 1 < layer_count:
            relays.append(relay_own_parity(layer + 1, spreads[layer + 1]))
        if layer + 1 < layer_count:
            attended = attend(layer, 0, peers, pl.ds(0, tokens))
            relays[layer + 1] += relay_partner(layer + 1, spreads[layer + 1])
            weight_copies[layer][1].wait()
            stream_in[...] = project(layer, 0, peers, attended)

    last = layer_count - 1
    weight_copies[last][1].wait()
    out_copies = []
    for turn, (owner, exchange) in enumerate(((1 - side, far), (side, near))):
        first_block = owner * half
        kept_rows = pl.ds(turn * half * tok_rows, half * tok_rows)
        attended = attend(last, first_block, half, kept_rows)
        finished[pl.ds(first_block, half)] = project(last, first_block, half, attended)
        for slot, target in exchange:
            copy = remote(
                finished.at[target],
                result.at[me],
                out_send.at[slot],
                out_recv.at[slot],
                (group, target, core),
            )
            copy.start()
            out_copies.append(copy)
    kept = pltpu.make_async_copy(finished.at[me], result.at[me], load_sem.at[6])
    kept.start()
    for copies in [stream_copies, bias_copies] + relays:
        for copy in copies:
            copy.wait_send()
    for copy in out_copies:
        copy.wait()
    kept.wait()


def particle_body(peers, states, ancestors, noise, pair, token_mask, w_qkv, w_out, w_pair):
    part_count, tok_rows, width = states.shape
    layer_count, _, head_count = w_pair.shape
    tokens = peers * tok_rows
    hbm = pl.BlockSpec(memory_space=pltpu.HBM)
    dma = pltpu.SemaphoreType.DMA
    per_peer, per_layer = dma((peers,)), dma((layer_count, peers))
    return pl.pallas_call(
        functools.partial(particle_kernel, peers, head_count),
        out_shape=jax.ShapeDtypeStruct(states.shape, states.dtype),
        in_specs=[hbm] * 8,
        out_specs=hbm,
        scratch_shapes=[
            pltpu.SMEM(ancestors.shape, ancestors.dtype),
            pltpu.VMEM(noise.shape, noise.dtype),
            pltpu.VMEM(pair.shape, pair.dtype),
            pltpu.VMEM((1, tokens), token_mask.dtype),
            pltpu.VMEM((layer_count, head_count, w_pair.shape[1]), w_pair.dtype),
            pltpu.VMEM((2 * part_count, tok_rows, width), jnp.bfloat16),
            pltpu.VMEM((peers, tok_rows, width), jnp.bfloat16),
            pltpu.VMEM((peers, tok_rows, width), jnp.bfloat16),
            pltpu.VMEM((layer_count, peers, head_count, tok_rows, tokens), jnp.bfloat16),
            pltpu.VMEM((head_count, tok_rows, tokens), jnp.float32),
            pltpu.VMEM((tokens, 3 * width), jnp.bfloat16),
            pltpu.VMEM((head_count * tokens, tokens), jnp.float32),
            pltpu.VMEM((tokens, head_count * tokens), jnp.bfloat16),
            pltpu.VMEM((peers, tok_rows, width), jnp.bfloat16),
            pltpu.VMEM(w_qkv.shape, w_qkv.dtype),
            pltpu.VMEM(w_out.shape, w_out.dtype),
            dma((7,)),
            dma((layer_count, 2)),
            dma((2, 2)),
            per_peer,
            per_peer,
            per_layer,
            per_layer,
            per_layer,
            per_layer,
            per_peer,
            per_peer,
        ],
        compiler_params=pltpu.CompilerParams(
            collective_id=0, has_side_effects=True, vmem_limit_bytes=63 * 1024 * 1024
        ),
        name="particle_layers",
    )(
        ancestors,
        states,
        noise,
        pair,
        token_mask.reshape(1, tokens),
        jnp.transpose(w_pair, (0, 2, 1)),
        w_qkv,
        w_out,
    )


def body(peers, states, ancestors, noise, pair, token_mask, w_qkv, w_out, w_pair):
    part_count, tok_rows, width = states.shape
    one_each = part_count == peers and peers % 2 == 0 and tok_rows % 16 == 0 and peers * tok_rows == LANES and width % LANES == 0
    inner = functools.partial(particle_body, peers) if one_each else token_split_body
    return inner(states, ancestors, noise, pair, token_mask, w_qkv, w_out, w_pair)


def solution(mesh):
    placed = (
        P(("groups", "dom"), "tok", None),
        P(("groups", "dom")),
        P(("groups", "dom"), "tok", None),
        P(("groups", "tok"), None, None),
        P("groups"),
        P(),
        P(),
        P(),
    )
    return jax.shard_map(
        functools.partial(body, mesh.shape["tok"]),
        mesh=mesh,
        in_specs=placed,
        out_specs=P(("groups", "dom"), "tok", None),
        check_vma=False,
    )
```

```python
import functools

import jax
import jax.numpy as jnp
from jax import lax
from jax.experimental import pallas as pl
from jax.experimental.pallas import tpu as pltpu
from jax.sharding import PartitionSpec as P


def layer_norm(stream):
    values = stream.astype(jnp.float32)
    average = jnp.mean(values, axis=-1, keepdims=True)
    centred = values - average
    spread = jnp.mean(centred * centred, axis=-1, keepdims=True)
    return centred * lax.rsqrt(spread + 1e-05)


def token_split_body(states, ancestors, noise, pair, token_mask, w_qkv, w_out, w_pair):
    part_count = states.shape[0]
    tok_rows = states.shape[1]
    model_width = states.shape[2]
    head_count = w_pair.shape[2]
    head_width = model_width // head_count
    layer_count = w_qkv.shape[0]
    total_keys = pair.shape[1]
    everyone = lax.all_gather(states, "dom", axis=0, tiled=True)
    chosen = jnp.take(everyone, ancestors, axis=0)
    stream = (chosen.astype(jnp.float32) + 0.5 * noise.astype(jnp.float32)).astype(jnp.bfloat16)
    penalty = jnp.where(token_mask > 0, 0.0, -1000000000.0).astype(jnp.float32)
    pair_terms = jnp.einsum("ijc,lch->lhij", pair, w_pair, preferred_element_type=jnp.float32)
    full_bias = pair_terms + penalty[None, None, None, :]
    query_scale = head_width ** (-0.5)
    for layer_index in range(layer_count):
        normed = layer_norm(stream).astype(jnp.bfloat16)
        projected = jnp.dot(
            normed.reshape(part_count * tok_rows, model_width),
            w_qkv[layer_index],
            preferred_element_type=jnp.float32,
        )
        projected = projected.reshape(part_count, tok_rows, 3 * model_width)
        query = (projected[..., :model_width] * query_scale).astype(jnp.bfloat16)
        key_tiles = projected[..., model_width : 2 * model_width].astype(jnp.bfloat16)
        value_tiles = projected[..., 2 * model_width :].astype(jnp.bfloat16)
        layer_bias = full_bias[layer_index]
        query_heads = query.reshape(part_count, tok_rows, head_count, head_width)
        all_keys, all_values = (
            lax.all_gather(key_tiles, "tok", axis=1, tiled=True),
            lax.all_gather(value_tiles, "tok", axis=1, tiled=True),
        )
        key_heads = all_keys.reshape(part_count, total_keys, head_count, head_width)
        scores = (
            jnp.einsum(
                "pihe,pjhe->phij", query_heads, key_heads, preferred_element_type=jnp.float32
            )
            + layer_bias[None]
        )
        weights = jax.nn.softmax(scores, axis=-1).astype(jnp.bfloat16)
        value_heads = all_values.reshape(part_count, total_keys, head_count, head_width)
        attended = jnp.einsum(
            "phij,pjhe->pihe", weights, value_heads, preferred_element_type=jnp.float32
        ).astype(jnp.bfloat16)
        attended = attended.reshape(part_count * tok_rows, model_width)
        update = jnp.dot(attended, w_out[layer_index], preferred_element_type=jnp.float32)
        update = update.reshape(part_count, tok_rows, model_width)
        stream = (stream.astype(jnp.float32) + update).astype(jnp.bfloat16)
    return stream


MESH = pl.DeviceIdType.MESH
LANES = 128


def particle_kernel(
    peers,
    head_count,
    ancestors_hbm,
    states,
    noise_hbm,
    pair_hbm,
    mask_hbm,
    w_pair_hbm,
    w_qkv_hbm,
    w_out_hbm,
    result,
    ancestors,
    noise,
    pair,
    token_mask,
    w_pair,
    everyone,
    outgoing,
    stream_in,
    bias,
    bias_rows,
    qkv,
    score_rows,
    raised,
    finished,
    w_qkv,
    w_out,
    load_sem,
    weight_sem,
    state_sem,
    stream_send,
    stream_recv,
    bias_send,
    bias_recv,
    relay_send,
    relay_recv,
    out_send,
    out_recv,
):
    group = lax.axis_index("groups")
    me = lax.axis_index("tok")
    core = lax.axis_index("dom")
    sibling = (group, me, 1 - core)
    part_count, tok_rows, width = states.shape
    layer_count = w_qkv.shape[0]
    tokens = peers * tok_rows
    head_width = width // head_count
    half_heads = head_count // 2

    def ahead(step):
        return lax.rem(me + step, peers)

    def behind(step):
        return lax.rem(me + peers - step, peers)

    half = peers // 2
    side, place_in_half = me // half, lax.rem(me, half)
    far = [
        (half + step, (1 - side) * half + lax.rem(place_in_half + step, half))
        for step in range(half)
    ]
    near = [
        (step, side * half + lax.rem(place_in_half + step, half)) for step in range(1, half)
    ]
    exchanges = near + far

    def remote(source, target, send, recv, device):
        return pltpu.make_async_remote_copy(
            src_ref=source,
            dst_ref=target,
            send_sem=send,
            recv_sem=recv,
            device_id=device,
            device_id_type=MESH,
        )

    weight_copies = []
    for layer in range(layer_count):
        weight_copies.append(
            (
                pltpu.make_async_copy(w_qkv_hbm.at[layer], w_qkv.at[layer], weight_sem.at[layer, 0]),
                pltpu.make_async_copy(w_out_hbm.at[layer], w_out.at[layer], weight_sem.at[layer, 1]),
            )
        )
    mine = pl.ds(core * part_count, part_count)
    loads = []
    for place, (source, target) in enumerate(
        (
            (pair_hbm, pair),
            (w_pair_hbm, w_pair),
            (mask_hbm, token_mask),
            (ancestors_hbm, ancestors),
            (states, everyone.at[mine]),
            (noise_hbm, noise),
        )
    ):
        loads.append(pltpu.make_async_copy(source, target, load_sem.at[place]))
        loads[-1].start()
    weight_copies[0][0].start()

    barrier = pltpu.get_barrier_semaphore()
    pl.semaphore_signal(barrier, inc=1, device_id=sibling, device_id_type=MESH)
    for step in range(1, peers):
        pl.semaphore_signal(
            barrier, inc=1, device_id=(group, ahead(step), core), device_id_type=MESH
        )
    def pair_product(layer):
        return lax.dot_general(
            w_pair[layer],
            pair[...].reshape(tok_rows * tokens, pair.shape[2]),
            (((1,), (1,)), ((), ())),
            preferred_element_type=jnp.float32,
        )
    for load in loads[:3]:
        load.wait()
    first_terms = pair_product(0)
    pl.semaphore_wait(barrier, peers)

    state_copies = []
    share = part_count // 2
    for piece in range(2):
        copy = remote(
            states.at[pl.ds(piece * share, share)],
            everyone.at[pl.ds(core * part_count + piece * share, share)],
            state_sem.at[0, piece],
            state_sem.at[1, piece],
            sibling,
        )
        copy.start()
        state_copies.append(copy)
    def make_bias(layer, pair_terms):
        penalty = jnp.where(token_mask[...] > 0, 0.0, -1000000000.0).astype(jnp.float32)
        for row in range(tok_rows):
            full = pair_terms[:, row * tokens : (row + 1) * tokens] + penalty
            bias_rows[:, row, :] = full - jnp.max(full, axis=-1, keepdims=True)
        bias[layer, me] = bias_rows[...].astype(jnp.bfloat16)

    my_heads = pl.ds(core * half_heads, half_heads)
    pairs = peers // 2
    partner = me + 1 - 2 * lax.rem(me, 2)
    bias_copies = []

    def send_bias(layer, slot, owner, target):
        block = bias.at[layer, owner, my_heads]
        copy = remote(
            block,
            block,
            bias_send.at[layer, slot],
            bias_recv.at[layer, slot],
            (group, target, core),
        )
        copy.start()
        bias_copies.append(copy)
        return copy

    def spread(layer):
        copies = [send_bias(layer, 0, me, partner)]
        for step in range(1, pairs):
            copies.append(send_bias(layer, step, me, ahead(2 * step)))
        return copies

    def hand_over(layer, slot, owner):
        block = bias.at[layer, owner, my_heads]
        copy = remote(
            block, block, relay_send.at[layer, slot], relay_recv.at[layer, slot], sibling
        )
        copy.start()
        return copy

    def relay_own_parity(layer, copies):
        handed = []
        for step in range(1, pairs):
            copies[step].wait_recv()
            copies.append(send_bias(layer, pairs - 1 + step, behind(2 * step), partner))
            handed.append(hand_over(layer, step, behind(2 * step)))
        copies[0].wait_recv()
        handed.append(hand_over(layer, 0, partner))
        return handed

    def relay_partner(layer, copies):
        handed = []
        for step in range(1, pairs):
            slot = pairs - 1 + step
            copies[slot].wait_recv()
            owner = lax.rem(partner + peers - 2 * step, peers)
            handed.append(hand_over(layer, slot, owner))
        return handed

    make_bias(0, first_terms)
    spreads = [spread(0)]
    relays = []

    for load in loads[3:]:
        load.wait()
    for copy in state_copies:
        copy.wait()

    def moved(particle):
        chosen = everyone[ancestors[particle]].astype(jnp.float32)
        return (chosen + 0.5 * noise[particle].astype(jnp.float32)).astype(jnp.bfloat16)

    stream_copies = []
    for step, target in exchanges:
        outgoing[step] = moved(target)
        copy = remote(
            outgoing.at[step],
            stream_in.at[me],
            stream_send.at[step],
            stream_recv.at[step],
            (group, target, core),
        )
        copy.start()
        stream_copies.append(copy)
    stream_in[me] = moved(me)
    for layer in range(layer_count):
        if layer > 0:
            weight_copies[layer][0].start()
        weight_copies[layer][1].start()

    for layer in range(1, layer_count):
        make_bias(layer, pair_product(layer))
    relays.append(relay_own_parity(0, spreads[0]))
    def head_lanes(head, start, size):
        lanes = lax.broadcasted_iota(jnp.int32, (1, size), 1) + start
        inside = (lanes >= head * head_width) & (lanes < (head + 1) * head_width)
        return jnp.where(inside, 1.0, 0.0).astype(jnp.bfloat16)

    def attend(layer, first_block, blocks, kept_rows):
        rows = blocks * tok_rows
        tiles = []
        ready = 0
        for tile in range(width // LANES):
            start = tile * LANES
            first = start // head_width
            last = (start + LANES + head_width - 1) // head_width
            for head in range(ready, last):
                first_score = pl.multiple_of(head * tokens + first_block * tok_rows, tok_rows)
                bias_block = bias[layer, pl.ds(first_block, blocks), head]
                scores = score_rows[pl.ds(first_score, rows)] + bias_block.reshape(
                    rows, tokens
                ).astype(jnp.float32)
                largest = jnp.max(scores, axis=-1, keepdims=True)
                raised[kept_rows, pl.ds(head * tokens, tokens)] = jnp.exp(scores - largest).astype(
                    jnp.bfloat16
                )
            ready = last
            value = qkv[:, pl.ds(2 * width + start, LANES)]
            masks = [
                jnp.broadcast_to(head_lanes(head, start, LANES), (tokens, LANES))
                for head in range(first, last)
            ]
            sides = jnp.concatenate(
                [jnp.concatenate([value * mask, mask], axis=1) for mask in masks], axis=0
            )
            part = jnp.dot(
                raised[kept_rows, pl.ds(first * tokens, (last - first) * tokens)],
                sides,
                preferred_element_type=jnp.float32,
            )
            tiles.append((part[:, :LANES] / part[:, LANES:]).astype(jnp.bfloat16))
        return jnp.concatenate(tiles, axis=1)

    def project(layer, first_block, blocks, attended):
        update = jnp.dot(attended, w_out[layer], preferred_element_type=jnp.float32)
        old = stream_in[pl.ds(first_block, blocks)].astype(jnp.float32)
        return (old + update.reshape(old.shape)).astype(jnp.bfloat16)

    def make_qkv(layer, first_block, blocks):
        rows = blocks * tok_rows
        first_row = first_block * tok_rows
        if blocks < peers:
            first_row = pl.multiple_of(first_row, rows)
        stream = stream_in[pl.ds(first_block, blocks)].reshape(rows, width)
        normed = layer_norm(stream).astype(jnp.bfloat16)
        for block in range(3):
            columns = pl.ds(block * width, width)
            projected = jnp.dot(
                normed, w_qkv[layer, :, columns], preferred_element_type=jnp.float32
            )
            if block == 0:
                projected = projected * head_width ** (-0.5)
            qkv[pl.ds(first_row, rows), columns] = projected.astype(jnp.bfloat16)

    windows = []
    for head in range(head_count):
        if windows and (head + 1) * head_width <= windows[-1][0] + 2 * LANES:
            windows[-1][1].append(head)
        else:
            start = head * head_width // LANES * LANES
            windows.append((min(start, width - 2 * LANES), [head]))

    for layer in range(layer_count):
        if layer == 0:
            for copy in stream_copies[: half - 1]:
                copy.wait_recv()
            weight_copies[0][0].wait()
            make_qkv(0, side * half, half)
            relays[0] += relay_partner(0, spreads[0])
            for copy in stream_copies[half - 1 :]:
                copy.wait_recv()
            if layer + 1 < layer_count:
                spreads.append(spread(layer + 1))
            make_qkv(0, (1 - side) * half, half)
        else:
            if layer + 1 < layer_count:
                spreads.append(spread(layer + 1))
            weight_copies[layer][0].wait()
            make_qkv(layer, 0, peers)
        for start, heads in windows:
            query = qkv[:, pl.ds(start, 2 * LANES)]
            score_rows[pl.ds(heads[0] * tokens, len(heads) * tokens)] = lax.dot_general(
                jnp.concatenate(
                    [query * head_lanes(head, start, 2 * LANES) for head in heads], axis=0
                ),
                qkv[:, pl.ds(width + start, 2 * LANES)],
                (((1,), (1,)), ((), ())),
                preferred_element_type=jnp.float32,
            )
        for copy in relays[layer]:
            copy.wait_recv()
        if layer + 1 < layer_count:
            relays.append(relay_own_parity(layer + 1, spreads[layer + 1]))
        if layer + 1 < layer_count:
            attended = attend(layer, 0, peers, pl.ds(0, tokens))
            relays[layer + 1] += relay_partner(layer + 1, spreads[layer + 1])
            weight_copies[layer][1].wait()
            stream_in[...] = project(layer, 0, peers, attended)

    last = layer_count - 1
    weight_copies[last][1].wait()
    out_copies = []
    for turn, (owner, exchange) in enumerate(((1 - side, far), (side, near))):
        first_block = owner * half
        kept_rows = pl.ds(turn * half * tok_rows, half * tok_rows)
        attended = attend(last, first_block, half, kept_rows)
        finished[pl.ds(first_block, half)] = project(last, first_block, half, attended)
        for slot, target in exchange:
            copy = remote(
                finished.at[target],
                result.at[me],
                out_send.at[slot],
                out_recv.at[slot],
                (group, target, core),
            )
            copy.start()
            out_copies.append(copy)
    kept = pltpu.make_async_copy(finished.at[me], result.at[me], load_sem.at[6])
    kept.start()
    for copies in [stream_copies, bias_copies] + relays:
        for copy in copies:
            copy.wait_send()
    for copy in out_copies:
        copy.wait()
    kept.wait()


def particle_body(peers, states, ancestors, noise, pair, token_mask, w_qkv, w_out, w_pair):
    part_count, tok_rows, width = states.shape
    layer_count, _, head_count = w_pair.shape
    tokens = peers * tok_rows
    hbm = pl.BlockSpec(memory_space=pltpu.HBM)
    dma = pltpu.SemaphoreType.DMA
    per_peer, per_layer = dma((peers,)), dma((layer_count, peers))
    return pl.pallas_call(
        functools.partial(particle_kernel, peers, head_count),
        out_shape=jax.ShapeDtypeStruct(states.shape, states.dtype),
        in_specs=[hbm] * 8,
        out_specs=hbm,
        scratch_shapes=[
            pltpu.SMEM(ancestors.shape, ancestors.dtype),
            pltpu.VMEM(noise.shape, noise.dtype),
            pltpu.VMEM(pair.shape, pair.dtype),
            pltpu.VMEM((1, tokens), token_mask.dtype),
            pltpu.VMEM((layer_count, head_count, w_pair.shape[1]), w_pair.dtype),
            pltpu.VMEM((2 * part_count, tok_rows, width), jnp.bfloat16),
            pltpu.VMEM((peers, tok_rows, width), jnp.bfloat16),
            pltpu.VMEM((peers, tok_rows, width), jnp.bfloat16),
            pltpu.VMEM((layer_count, peers, head_count, tok_rows, tokens), jnp.bfloat16),
            pltpu.VMEM((head_count, tok_rows, tokens), jnp.float32),
            pltpu.VMEM((tokens, 3 * width), jnp.bfloat16),
            pltpu.VMEM((head_count * tokens, tokens), jnp.float32),
            pltpu.VMEM((tokens, head_count * tokens), jnp.bfloat16),
            pltpu.VMEM((peers, tok_rows, width), jnp.bfloat16),
            pltpu.VMEM(w_qkv.shape, w_qkv.dtype),
            pltpu.VMEM(w_out.shape, w_out.dtype),
            dma((7,)),
            dma((layer_count, 2)),
            dma((2, 2)),
            per_peer,
            per_peer,
            per_layer,
            per_layer,
            per_layer,
            per_layer,
            per_peer,
            per_peer,
        ],
        compiler_params=pltpu.CompilerParams(
            collective_id=0, has_side_effects=True, vmem_limit_bytes=63 * 1024 * 1024
        ),
        name="particle_layers",
    )(
        ancestors,
        states,
        noise,
        pair,
        token_mask.reshape(1, tokens),
        jnp.transpose(w_pair, (0, 2, 1)),
        w_qkv,
        w_out,
    )


def body(peers, states, ancestors, noise, pair, token_mask, w_qkv, w_out, w_pair):
    part_count, tok_rows, width = states.shape
    one_each = part_count == peers and peers % 2 == 0 and tok_rows % 16 == 0 and peers * tok_rows == LANES and width % LANES == 0
    inner = functools.partial(particle_body, peers) if one_each else token_split_body
    return inner(states, ancestors, noise, pair, token_mask, w_qkv, w_out, w_pair)


def solution(mesh):
    placed = (
        P(("groups", "dom"), "tok", None),
        P(("groups", "dom")),
        P(("groups", "dom"), "tok", None),
        P(("groups", "tok"), None, None),
        P("groups"),
        P(),
        P(),
        P(),
    )
    return jax.shard_map(
        functools.partial(body, mesh.shape["tok"]),
        mesh=mesh,
        in_specs=placed,
        out_specs=P(("groups", "dom"), "tok", None),
        check_vma=False,
    )
```
